128 devices in a mesh: seg: 4 (over x), sec: 32 (over z, y, core).
Axes of the slice: x: 4, y: 4, z: 4, core: 2. Of those that a mesh axis runs over, the one named last changes fastest.
Arguments:
- left_env: bfloat16 [4, 32, 13, 512, 512], P('seg', 'sec'), may hold values from -0.25 to 0.25
- right_env: bfloat16 [4, 32, 13, 512, 512], P('seg', 'sec'), may hold values from -0.25 to 0.25
- left_block: bfloat16 [4, 32, 512, 512], P('seg', 'sec'), may hold values from -8 to 8
- right_block: bfloat16 [4, 32, 512, 512], P('seg', 'sec'), may hold values from -0.25 to 0.25
- inv_sv: bfloat16 [4, 32, 512], P('seg', 'sec'), may hold values from 0.5 to 2
- precond: float32 [4, 32, 512, 512], P('seg', 'sec'), may hold values from 1 to 4
- sector_dims: int32 [4, 32, 2], P('seg', 'sec'), may hold values from 128 to 512, as said below
- channel_charge: int32 [13], replicated, may hold values from -1 to 1
Outputs:
- next_vector: bfloat16 [4, 32, 512, 512], P('seg', 'sec')
- last_image: float32 [4, 32, 512, 512], P('seg', 'sec')
- projected: float32 [4, 4, 4], P('seg')
The draws below stay inside these ranges and needn't reach their ends.
Inputs may be any that keep to these rules, and one draw needn't show every extreme that they name: `sector_dims`: in every segment some sector has left bond dimension 512 and some sector has right bond dimension 512.
All inputs are finite; a program needn't handle non-finite values.
Results may differ from the reference program's by a relative error of at most 0.024.
Values may be sent and summed in bfloat16 or wider, within the bound.
No kernel may reach another device: no remote copies, remote signals or barrier semaphores. Data moves between devices by JAX's collectives and lax.ppermute only.
A program may use at most 64 MiB of HBM per device.

```python
import math
import jax
import jax.numpy as jnp
from jax import lax

M = 512
W = 13
MATVECS = 4
SEGS = 4
SECTORS = 32


def draw_sector_dims(key, part):
    first_key, second_key = jax.random.split(jax.random.fold_in(key, 7))
    dims = jax.random.randint(first_key, (SEGS, SECTORS, 2), M // 4, M + 1)
    picked = jax.random.randint(second_key, (SEGS, 2), 0, SECTORS)
    hit = jnp.arange(SECTORS)[None, :, None] == picked[:, None, :]
    return jnp.where(hit, M, dims).astype(jnp.int32)


def draw_left_block(key, part):
    inner_key = jax.random.fold_in(key, 11)
    position = jnp.arange(SECTORS, dtype=jnp.float32) / max(SECTORS - 1, 1)
    factor = jnp.exp(jnp.log(0.4) + position * jnp.log(5.0))
    values = jax.random.normal(inner_key, (SEGS, SECTORS, M, M), jnp.float32)
    return jnp.clip(values * factor[None, :, None, None], -8.0, 8.0).astype(jnp.bfloat16)


def plant(drawn, stream_key, low, high):
    longest = drawn.shape.index(max(drawn.shape))
    spots = []
    for shift in (0, 1):
        where = [jax.random.randint(jax.random.fold_in(stream_key, axis), (), 0, length) for axis, length in enumerate(drawn.shape)]
        where[longest] = (where[longest] + shift) % drawn.shape[longest]
        spots.append(tuple(where))
    return drawn.at[spots[0]].set(low).at[spots[1]].set(high)


def steps_of(stream_key, shape, cuts, low, largest):
    def one(axis_at, shards_of):
        steps = jax.random.uniform(jax.random.fold_in(jax.random.fold_in(stream_key, 6), axis_at), (shards_of,), jnp.float32, low / len(cuts), largest / len(cuts))
        return jnp.repeat(jnp.exp(steps), shape[axis_at] // shards_of).reshape((-1,) + (1,) * (len(shape) - axis_at - 1))

    gain = one(*cuts[0])
    for cut in cuts[1:]:
        gain = gain * one(*cut)
    return gain


def gaussian(stream_key, shape, width, bound, cuts=(), kind=jnp.bfloat16):
    values = width * jax.random.normal(stream_key, shape, jnp.float32)
    if cuts:
        values = values * steps_of(stream_key, shape, cuts, -0.22, 0.18)
    return jnp.clip(values, -bound, bound).astype(kind)


def setup_inputs(seed: int = 0) -> dict:
    splits = jax.random.split(jax.random.key(seed), 9)
    return {
        "left_env": gaussian(splits[0], (SEGS, SECTORS, W, M, M), M ** -0.5, 0.25, ((0, 4), (1, 32))),
        "right_env": gaussian(splits[1], (SEGS, SECTORS, W, M, M), M ** -0.5, 0.25, ((0, 4), (1, 32))),
        "left_block": draw_left_block(jax.random.fold_in(splits[8], 71), 0),
        "right_block": gaussian(splits[3], (SEGS, SECTORS, M, M), M ** -0.5, 0.25, ((0, 4), (1, 32))),
        "inv_sv": jnp.clip(jnp.exp(math.log(2.0) - 1.3862944 * jax.random.uniform(splits[4], (SEGS, SECTORS, M), jnp.float32) ** steps_of(splits[4], (SEGS, SECTORS, M), ((0, 4), (1, 32)), -0.2, 0.2)), 0.5, 2.0).astype(jnp.bfloat16),
        "precond": jnp.clip(jnp.exp(math.log(4.0) - 1.3862944 * jax.random.uniform(splits[5], (SEGS, SECTORS, M, M), jnp.float32) ** steps_of(splits[5], (SEGS, SECTORS, M, M), ((0, 4), (1, 32)), -0.2, 0.2)), 1.0, 4.0),
        "sector_dims": draw_sector_dims(jax.random.fold_in(splits[8], 71), 0),
        "channel_charge": plant(jax.random.randint(splits[7], (W,), -1, 2), jax.random.fold_in(splits[7], 1), -1, 1).astype(jnp.int32),
    }


def reference(left_env, right_env, left_block, right_block, inv_sv, precond, sector_dims, channel_charge):
    eps = 1e-06
    index = jnp.arange(M, dtype=jnp.int32)
    mask = ((index[None, None, :, None] < sector_dims[:, :, 0, None, None]) & (index[None, None, None, :] < sector_dims[:, :, 1, None, None])).astype(jnp.float32)
    count = SECTORS * M * M

    def inner(first, second):
        return lax.optimization_barrier(jnp.sum(first * second, axis=(1, 2, 3))) / count

    def expand(value):
        return value[:, None, None, None]
    neighbour_block = jnp.roll(right_block, -1, axis=0)
    neighbour_inv = jnp.roll(inv_sv, -1, axis=0)
    scaled = (left_block.astype(jnp.float32) * neighbour_inv.astype(jnp.float32)[:, :, None, :]).astype(jnp.bfloat16)
    guess = jnp.einsum('gsab,gsbc->gsac', scaled.astype(jnp.float32), neighbour_block.astype(jnp.float32)) * mask
    first = (guess * expand(lax.rsqrt(inner(guess, guess) + eps))).astype(jnp.bfloat16)
    select = (channel_charge[:, None] == jnp.array([-1, 0, 1], dtype=jnp.int32)[None, :]).astype(jnp.float32)
    left_flat = left_env.reshape(SEGS * SECTORS, W, M, M)
    right_flat = right_env.reshape(SEGS * SECTORS, W, M, M)

    def apply(vector):
        vector_flat = vector.reshape(SEGS * SECTORS, M, M)

        def single(pieces):
            left_one, right_one, vec_one = pieces
            left_x = jnp.einsum('wab,bc->wac', left_one.astype(jnp.float32), vec_one.astype(jnp.float32)).astype(jnp.bfloat16)
            terms = jnp.einsum('wac,wdc->wad', left_x.astype(jnp.float32), right_one.astype(jnp.float32))
            return jnp.stack([lax.optimization_barrier(jnp.sum(terms * select[:, q, None, None], axis=0)) for q in range(3)])
        grouped = lax.map(single, (left_flat, right_flat, vector_flat)).reshape(SEGS, SECTORS, 3, M, M)
        to_lower = grouped[:, :, 0]
        stay = grouped[:, :, 1]
        to_upper = grouped[:, :, 2]
        zero = jnp.zeros_like(stay[:, :1])
        from_lower = jnp.concatenate([zero, to_upper[:, :-1]], axis=1)
        from_upper = jnp.concatenate([to_lower[:, 1:], zero], axis=1)
        return (stay + from_lower + from_upper) * mask
    basis = [first]
    columns = []
    image = None
    for step in range(MATVECS):
        current = basis[step]
        image = apply(current)
        column = [inner(basis[j].astype(jnp.float32), image) for j in range(step + 1)]
        column = column + [jnp.zeros((SEGS,), jnp.float32) for j in range(MATVECS - step - 1)]
        columns.append(jnp.stack(column, axis=1))
        theta = column[step]
        resid = image - expand(theta) * current.astype(jnp.float32)
        correction = resid / precond
        projected_part = jnp.zeros_like(correction)
        for j in range(step + 1):
            weight = inner(basis[j].astype(jnp.float32), correction)
            projected_part = projected_part + expand(weight) * basis[j].astype(jnp.float32)
        remain = correction - projected_part
        basis.append((remain * expand(lax.rsqrt(inner(remain, remain) + eps))).astype(jnp.bfloat16))
    projected = jnp.stack(columns, axis=2)
    return (basis[-1], image, projected)
```

```python
import jax
import jax.numpy as jnp
from jax import lax
from jax.sharding import PartitionSpec as P

MATVECS = 4
EPS = 1e-06


def shifted(block, axis, distance):
    devices = range(lax.axis_size(axis))
    route = [((i - distance) % len(devices), i) for i in devices]
    return lax.ppermute(block, axis, route)


def shifted_2(x, axis, by):
    count = lax.axis_size(axis)
    pairs = [(i, i + by) for i in range(count) if 0 <= i + by < count]
    return lax.ppermute(x, axis, pairs)


def total(values, axis):
    row = jnp.stack(values + [jnp.zeros((), jnp.float32)] * (128 - len(values)))
    spread = jnp.broadcast_to(row[None, None], (lax.axis_size(axis), 1, 128))
    got = lax.all_to_all(spread, axis, 0, 0)
    summed = jnp.sum(got, axis=(0, 1))
    return [summed[i] for i in range(len(values))]


def per_device(
    left_env, right_env, left_block, right_block, inv_sv, precond, sector_dims, channel_charge
):
    width = left_block.shape[-1]
    count = lax.axis_size("sec") * width * width
    lenv = left_env[0, 0]
    renv = right_env[0, 0]
    dims = sector_dims[0, 0]
    inverse = 1.0 / precond[0, 0]
    index = jnp.arange(width, dtype=jnp.int32)
    mask = ((index[:, None] < dims[0]) & (index[None, :] < dims[1])).astype(jnp.float32)
    neighbour_block, neighbour_inv = shifted((right_block[0, 0], inv_sv[0, 0]), "seg", -1)
    scaled = (
        left_block[0, 0].astype(jnp.float32) * neighbour_inv.astype(jnp.float32)[None, :]
    ).astype(jnp.bfloat16)
    guess = jnp.dot(scaled, neighbour_block, preferred_element_type=jnp.float32) * mask

    def dot(first, second):
        return jnp.sum(first * second) / count

    select = (channel_charge[:, None] == jnp.array([-1, 0, 1], dtype=jnp.int32)[None, :]).astype(
        jnp.float32
    )
    basis = [guess.astype(jnp.bfloat16)]
    floats = [basis[0].astype(jnp.float32)]
    scales = []
    gram = {}
    columns = []
    for k in range(MATVECS):
        current = basis[k]
        left_x = jnp.einsum(
            "wab,bc->wac", lenv, current, preferred_element_type=jnp.float32
        ).astype(jnp.bfloat16)
        terms = jnp.einsum("wac,wdc->wad", left_x, renv, preferred_element_type=jnp.float32)
        to_lower = jnp.sum(terms * select[:, 0, None, None], axis=0)
        stay = jnp.sum(terms * select[:, 1, None, None], axis=0)
        to_upper = jnp.sum(terms * select[:, 2, None, None], axis=0)
        from_lower = shifted_2(to_upper.astype(jnp.bfloat16), "sec", 1).astype(to_upper.dtype)
        from_upper = shifted_2(to_lower.astype(jnp.bfloat16), "sec", -1).astype(to_lower.dtype)
        image = (stay + from_lower + from_upper) * mask
        a = image * inverse
        e = floats[k] * inverse
        steps = range(k + 1)
        values = [dot(floats[j], image) for j in steps]
        values += [dot(floats[j], a) for j in steps]
        values += [dot(floats[j], e) for j in steps]
        values += [dot(floats[j], floats[k]) for j in steps]
        values += [dot(a, a), dot(a, e), dot(e, e)]
        if k == 0:
            values.append(dot(guess, guess))
        values = total(values, "sec")
        n = k + 1
        hv, ha, he, hx = (values[i * n : (i + 1) * n] for i in range(4))
        aa, ae, ee = values[4 * n : 4 * n + 3]
        scales.append(lax.rsqrt(values[-1] + EPS) if k == 0 else jnp.ones((), jnp.float32))
        s = scales[k]
        column = [scales[j] * s * hv[j] for j in steps]
        columns.append(
            jnp.stack(column + [jnp.zeros((), jnp.float32) for j in range(MATVECS - n)])
        )
        theta = column[k]
        for j in steps:
            gram[j, k] = gram[k, j] = scales[j] * s * hx[j]
        d = [scales[j] * s * (ha[j] - theta * he[j]) for j in steps]
        cc = s * s * (aa - 2.0 * theta * ae + theta * theta * ee)
        pp = cc - 2.0 * sum(x * x for x in d)
        pp = pp + sum(d[i] * d[j] * gram[i, j] for i in steps for j in steps)
        norm = lax.rsqrt(jnp.maximum(pp, 0.0) + EPS)
        remain = s * (a - theta * e)
        for j in steps:
            remain = remain - (d[j] * scales[j]) * floats[j]
        following = (remain * norm).astype(jnp.bfloat16)
        basis.append(following)
        floats.append(following.astype(jnp.float32))
    projected = jnp.stack(columns, axis=1)
    return (basis[-1][None, None], (image * scales[-1])[None, None], projected[None])


def solution(mesh):
    in_specs = (
        P("seg", "sec", None, None, None),
        P("seg", "sec", None, None, None),
        P("seg", "sec", None, None),
        P("seg", "sec", None, None),
        P("seg", "sec", None),
        P("seg", "sec", None, None),
        P("seg", "sec", None),
        P(),
    )
    out_specs = (P("seg", "sec", None, None), P("seg", "sec", None, None), P("seg", None, None))
    return jax.shard_map(
        per_device, mesh=mesh, in_specs=in_specs, out_specs=out_specs, check_vma=False
    )
```

```python
import functools

import jax
import jax.numpy as jnp
from jax import lax
from jax.experimental import pallas as pl
from jax.experimental.pallas import tpu as pltpu
from jax.sharding import PartitionSpec as P

MATVECS = 4
EPS = 1e-06
ROWS = 64
MIB = 1 << 20
BF16 = jnp.bfloat16
F32 = jnp.float32
HV, HA, HE, HX, AA, AE, EE, UU = 0, 4, 8, 12, 16, 17, 18, 19

VMEM = pl.BlockSpec(memory_space=pltpu.VMEM)
SMEM = pl.BlockSpec(memory_space=pltpu.SMEM)
HBM = pl.BlockSpec(memory_space=pltpu.HBM)


def env_copies(slot, channel, refs):
    l_hbm, r_hbm, l_buf, r_buf, sems = refs
    return (
        pltpu.make_async_copy(l_hbm.at[channel], l_buf.at[slot], sems.at[slot, 0]),
        pltpu.make_async_copy(r_hbm.at[channel], r_buf.at[slot], sems.at[slot, 1]),
    )


def list_channels(charge, wanted, picked, count):
    def body(w, n):
        hit = charge[w] == wanted

        @pl.when(hit)
        def _():
            picked[n] = w

        return n + hit.astype(jnp.int32)

    return lax.fori_loop(0, charge.shape[0], body, count)


def apply_channels(picked, count, split, x_ref, t_ref, acc, l_ref, r_ref):
    acc[...] = jnp.zeros_like(acc)

    def body(i, carry):
        apply_one(l_ref, r_ref, picked[i], x_ref, t_ref, acc, (i >= split).astype(jnp.int32))
        return carry

    lax.fori_loop(0, count, body, 0)


def apply_one(l_ref, r_ref, w, x_ref, t_ref, acc, side):
    t_ref[...] = jnp.dot(l_ref[w], x_ref[...], preferred_element_type=F32).astype(BF16)
    acc[side] += lax.dot_general(
        t_ref[...], r_ref[w], (((1,), (1,)), ((), ())), preferred_element_type=F32
    )


def stream_channels(picked, count, x_ref, t_ref, acc, refs):
    acc[...] = jnp.zeros_like(acc)

    def body(i, carry):
        for copy in env_copies(i, picked[i], refs):
            copy.wait()
        apply_one(refs[2], refs[3], i, x_ref, t_ref, acc, 0)
        return carry

    lax.fori_loop(0, count, body, 0)


def mask_of(dims, rows, width, first=0):
    a = lax.broadcasted_iota(jnp.int32, (rows, width), 0) + first
    b = lax.broadcasted_iota(jnp.int32, (rows, width), 1)
    return (a < dims[0]) & (b < dims[1])


def fold(x):
    return jnp.sum(x.reshape(x.shape[0] // 8, 8, x.shape[1]), axis=0)


def lanes_of(values, lanes):
    lane = lax.broadcasted_iota(jnp.int32, (8, 128), 1)
    out = jnp.zeros((8, 128), F32)
    for value, at in zip(values, lanes):
        whole = jnp.sum(jnp.sum(value, axis=0, keepdims=True), axis=1, keepdims=True)
        out = jnp.where(lane == at, whole, out)
    return out


def first_kernel(
    charge, dims, far, lb, nb, inv, l_hbm, r_hbm, x_ref, far_ref, uu_ref,
    picked, t_ref, acc, l_buf, r_buf, sems,
):
    refs = (l_hbm, r_hbm, l_buf, r_buf, sems)
    count = list_channels(charge, far[0], picked, 0)

    def start(i, carry):
        for copy in env_copies(i, picked[i], refs):
            copy.start()
        return carry

    lax.fori_loop(0, count, start, 0)
    scaled = (lb[...].astype(F32) * inv[...].astype(F32)).astype(BF16)
    guess = jnp.dot(scaled, nb[...], preferred_element_type=F32)
    guess = jnp.where(mask_of(dims, *guess.shape), guess, 0.0)
    x_ref[...] = guess.astype(BF16)
    uu_ref[...] = lanes_of([fold(guess * guess)], [UU])
    stream_channels(picked, count, x_ref, t_ref, acc, refs)
    far_ref[...] = acc[0].astype(BF16)


def at(red, lane):
    return red[0:1, lane : lane + 1]


def scales_of(reds):
    return [lax.rsqrt(at(reds[0], UU) + EPS)] + [jnp.ones((1, 1), F32)] * (len(reds) - 1)


def solve_step(reds):
    k = len(reds) - 1
    s = scales_of(reds)
    red = reds[k]
    steps = range(k + 1)
    gram = {}
    for i in steps:
        for j in range(i + 1):
            gram[i, j] = gram[j, i] = s[i] * s[j] * at(reds[i], HX + j)
    column = [s[j] * s[k] * at(red, HV + j) for j in steps]
    theta = column[k]
    d = [s[j] * s[k] * (at(red, HA + j) - theta * at(red, HE + j)) for j in steps]
    cc = s[k] * s[k] * (at(red, AA) - 2.0 * theta * at(red, AE) + theta * theta * at(red, EE))
    pp = cc
    for i in steps:
        pp = pp - 2.0 * d[i] * d[i]
        for j in steps:
            pp = pp + d[i] * d[j] * gram[i, j]
    norm = lax.rsqrt(jnp.maximum(pp, 0.0) + EPS)
    return column, norm * s[k], norm * s[k] * theta, [norm * d[j] * s[j] for j in steps]


def following(reds, image, inverse, basis, out):
    _, w_v, w_x, w = solve_step(reds)
    k = len(reds) - 1

    def body(block, carry):
        rows = pl.ds(block * ROWS, ROWS)
        xs = [b[rows, :].astype(F32) for b in basis]
        p = (image[rows, :] * w_v - xs[k] * w_x) * inverse[rows, :]
        for j in range(k + 1):
            p = p - xs[j] * w[j]
        out[rows, :] = p.astype(BF16)
        return carry

    lax.fori_loop(0, out.shape[0] // ROWS, body, 0)


def next_kernel(k, scale, *refs):
    charge, far, got = refs[:3]
    older = refs[3 : 3 + k - 1]
    basis = refs[2 + k : 2 + 2 * k]
    (
        image, inverse, l_ref, r_ref, x_ref, far_ref, red_ref,
        picked, t_ref, acc,
    ) = refs[2 + 2 * k :]
    count = list_channels(charge, far[0], picked, 0)
    red_ref[...] = jnp.sum(got[...], axis=0) * scale
    reds = [r[...] for r in older] + [red_ref[...]]
    following(reds, image, inverse, basis, x_ref)
    apply_channels(picked, count, count, x_ref, t_ref, acc, l_ref, r_ref)
    far_ref[...] = acc[0].astype(BF16)


def last_kernel(scale, *refs):
    k = MATVECS
    got = refs[0]
    older = refs[1:k]
    basis = refs[k : 2 * k]
    image, inverse, x_ref, projected = refs[2 * k :]
    reds = [r[...] for r in older] + [jnp.sum(got[...], axis=0) * scale]
    following(reds, image, inverse, basis, x_ref)
    row = lax.broadcasted_iota(jnp.int32, (MATVECS, MATVECS), 0)
    col = lax.broadcasted_iota(jnp.int32, (MATVECS, MATVECS), 1)
    out = jnp.zeros((MATVECS, MATVECS), F32)
    for step in range(MATVECS):
        column = solve_step(reds[: step + 1])[0]
        for j in range(step + 1):
            out = jnp.where((row == j) & (col == step), column[j], out)
    projected[...] = out


def rest_kernel(k, charge, far, *refs):
    basis = refs[: k + 1]
    precond, l_ref, r_ref = refs[k + 1 : k + 4]
    outs = refs[k + 4 :]
    if k == 0:
        near_ref, stay_ref, dots_ref, inverse, *scratch = outs
    else:
        near_ref, stay_ref, dots_ref, *scratch = outs
        inverse = precond
    picked, t_ref, acc = scratch
    split = list_channels(charge, -far[0], picked, 0)
    count = list_channels(charge, 0, picked, split)
    width = near_ref.shape[1]

    def body(block, sums):
        rows = pl.ds(block * ROWS, ROWS)
        if k == 0:
            inverse[rows, :] = 1.0 / precond[rows, :]
        xs = [b[rows, :].astype(F32) for b in basis]
        e = xs[k] * inverse[rows, :]
        new = [x * e for x in xs] + [x * xs[k] for x in xs] + [e * e]
        return tuple(total + fold(x) for total, x in zip(sums, new))

    zero = tuple(jnp.zeros((8, width), F32) for _ in range(2 * k + 3))
    sums = lax.fori_loop(0, near_ref.shape[0] // ROWS, body, zero)
    lanes = [HE + j for j in range(k + 1)] + [HX + j for j in range(k + 1)] + [EE]
    dots_ref[...] = lanes_of(sums, lanes)
    apply_channels(picked, count, split, basis[k], t_ref, acc, l_ref, r_ref)
    near_ref[...] = acc[0].astype(BF16)
    stay_ref[...] = acc[1]


def image_kernel(k, dims, *refs):
    basis = refs[: k + 1]
    stay, from_far, from_near, inverse, dots = refs[k + 1 : k + 6]
    rest = refs[k + 6 :]
    if k == 0:
        guess_dots, image, out = rest
    else:
        image, out = rest
    width = stay.shape[1]

    def body(block, sums):
        rows = pl.ds(block * ROWS, ROWS)
        v = stay[rows, :] + (from_far[rows, :].astype(F32) + from_near[rows, :].astype(F32))
        v = jnp.where(mask_of(dims, ROWS, width, block * ROWS), v, 0.0)
        image[rows, :] = v
        xs = [b[rows, :].astype(F32) for b in basis]
        d = inverse[rows, :]
        a = v * d
        e = xs[k] * d
        new = [x * v for x in xs] + [x * a for x in xs] + [a * a, a * e]
        return tuple(total + fold(x) for total, x in zip(sums, new))

    zero = tuple(jnp.zeros((8, width), F32) for _ in range(2 * k + 4))
    sums = lax.fori_loop(0, stay.shape[0] // ROWS, body, zero)
    lanes = [HV + j for j in range(k + 1)] + [HA + j for j in range(k + 1)] + [AA, AE]
    total = lanes_of(sums, lanes) + dots[...]
    if k == 0:
        total = total + guess_dots[...]
    out[...] = jnp.broadcast_to(total[None], out.shape)


def env_scratch(channels, width, sides):
    return [
        pltpu.SMEM((channels,), jnp.int32),
        pltpu.VMEM((width, width), BF16),
        pltpu.VMEM((sides, width, width), F32),
    ]


def call(kernel, args, specs, outs, scratch, flops, limit):
    return pl.pallas_call(
        kernel,
        out_shape=[jax.ShapeDtypeStruct(*o) for o in outs],
        in_specs=specs,
        out_specs=[VMEM] * len(outs),
        scratch_shapes=scratch,
        compiler_params=pltpu.CompilerParams(vmem_limit_bytes=limit * MIB),
        cost_estimate=pl.CostEstimate(
            flops=flops, bytes_accessed=4 * MIB + flops // 512, transcendentals=0
        ),
    )(*args)


def swapped(block, pairs):
    return lax.ppermute(block, "sec", pairs)


def per_device(
    left_env, right_env, left_block, right_block, inv_sv, precond, sector_dims, channel_charge
):
    width = left_block.shape[-1]
    sectors = lax.axis_size("sec")
    segments = lax.axis_size("seg")
    channels = left_env.shape[2]
    scale = 1.0 / (sectors * width * width)
    lenv, renv = left_env[0, 0], right_env[0, 0]
    dims, weights = sector_dims[0, 0], precond[0, 0]
    odd = lax.rem(lax.axis_index("sec"), 2)
    far = (2 * odd - 1).astype(jnp.int32).reshape(1)
    far_pairs = [(i, i + 1) for i in range(1, sectors - 1, 2)]
    far_pairs += [(j, i) for i, j in far_pairs]
    near_pairs = [(i, i + 1) for i in range(0, sectors, 2)]
    near_pairs += [(j, i) for i, j in near_pairs]
    route = [((i + 1) % segments, i) for i in range(segments)]
    nb, inv = lax.ppermute((right_block[0, 0], inv_sv[0]), "seg", route)

    in_hbm = [pltpu.with_memory_space_constraint(x, pltpu.HBM) for x in (lenv, renv)]
    square = (width, width)
    small = ((8, 128), F32)
    one = 4 * width**3 * channels // 3
    basis, reds = [], []
    for k in range(MATVECS):
        scratch = env_scratch(channels, width, 1)
        buffers = [pltpu.VMEM(lenv.shape, BF16)] * 2 + [pltpu.SemaphoreType.DMA((channels, 2))]
        if k == 0:
            x, to_far, guess_dots = call(
                first_kernel,
                (channel_charge, dims, far, left_block[0, 0], nb, inv, *in_hbm),
                [SMEM] * 3 + [VMEM] * 3 + [HBM] * 2,
                [(square, BF16), (square, BF16), small],
                scratch + buffers, one, 24,
            )
        else:
            x, to_far, red = call(
                functools.partial(next_kernel, k, scale),
                (channel_charge, far, got, *reds, *basis, image, inverse, lenv, renv),
                [SMEM] * 2 + [VMEM] * (2 * k + 2) + [VMEM] * 2,
                [(square, BF16), (square, BF16), small],
                scratch, one, 16,
            )
            reds.append(red)
        basis.append(x)
        from_far = swapped(to_far, far_pairs)
        outs = [(square, BF16), (square, F32), small]
        to_near, stay, dots, *new = call(
            functools.partial(rest_kernel, k),
            (channel_charge, far, *basis, weights if k == 0 else inverse, lenv, renv),
            [SMEM] * 2 + [VMEM] * (k + 2) + [VMEM] * 2,
            outs + ([(square, F32)] if k == 0 else []),
            env_scratch(channels, width, 2), 2 * one, 16,
        )
        if k == 0:
            inverse = new[0]
        from_near = swapped(to_near, near_pairs)
        extra = (guess_dots,) if k == 0 else ()
        image, spread = call(
            functools.partial(image_kernel, k),
            (dims, *basis, stay, from_far, from_near, inverse, dots, *extra),
            [SMEM] + [VMEM] * (k + 6 + len(extra)),
            [(square, F32), ((sectors, 8, 128), F32)],
            [], MIB, 16,
        )
        got = lax.all_to_all(spread, "sec", 0, 0)
    x, projected = call(
        functools.partial(last_kernel, scale),
        (got, *reds, *basis, image, inverse),
        [VMEM] * (2 * MATVECS + 2),
        [(square, BF16), ((MATVECS, MATVECS), F32)],
        [], MIB, 16,
    )
    return (x[None, None], image[None, None], projected[None])


def solution(mesh):
    in_specs = (
        P("seg", "sec", None, None, None),
        P("seg", "sec", None, None, None),
        P("seg", "sec", None, None),
        P("seg", "sec", None, None),
        P("seg", "sec", None),
        P("seg", "sec", None, None),
        P("seg", "sec", None),
        P(),
    )
    out_specs = (P("seg", "sec", None, None), P("seg", "sec", None, None), P("seg", None, None))
    return jax.shard_map(
        per_device, mesh=mesh, in_specs=in_specs, out_specs=out_specs, check_vma=False
    )
```

```python
import functools

import jax
import jax.numpy as jnp
from jax import lax
from jax.experimental import pallas as pl
from jax.experimental.pallas import tpu as pltpu
from jax.sharding import PartitionSpec as P

MATVECS = 4
EPS = 1e-06
ROWS = 64
ROW = 1
MIB = 1 << 20
BF16 = jnp.bfloat16
F32 = jnp.float32
HV, HA, HE, HX, AA, AE, EE, UU = 0, 4, 8, 12, 16, 17, 18, 19

VMEM = pl.BlockSpec(memory_space=pltpu.VMEM)
SMEM = pl.BlockSpec(memory_space=pltpu.SMEM)
HBM = pl.BlockSpec(memory_space=pltpu.HBM)


def env_copies(slot, channel, refs):
    l_hbm, r_hbm, l_buf, r_buf, sems = refs
    return (
        pltpu.make_async_copy(l_hbm.at[channel], l_buf.at[slot], sems.at[slot, 0]),
        pltpu.make_async_copy(r_hbm.at[channel], r_buf.at[slot], sems.at[slot, 1]),
    )


def apply_channels(picked, first, last, x_ref, t_ref, acc, l_ref, r_ref, arrived=None):
    def lefts(i, slot):
        w = picked[i] if arrived is None else arrived(i)
        t_ref[slot] = jnp.dot(l_ref[w], x_ref[...], preferred_element_type=F32).astype(BF16)
        return w

    def term(w, slot):
        return lax.dot_general(
            t_ref[slot], r_ref[w], (((1,), (1,)), ((), ())), preferred_element_type=F32
        )

    def pair(h, carry):
        one = lefts(first + 2 * h, 0)
        two = lefts(first + 2 * h + 1, 1)
        acc[...] += term(one, 0) + term(two, 1)
        return carry

    count = last - first
    lax.fori_loop(0, lax.div(count, 2), pair, 0)

    @pl.when(lax.rem(count, 2) == 1)
    def _():
        acc[...] += term(lefts(last - 1, 0), 0)


def prepare_kernel(charge, far, dims, lb, precond, lb_out, inverse, plan, sems):
    copies = [
        pltpu.make_async_copy(lb, lb_out, sems.at[0]),
        pltpu.make_async_copy(precond, inverse, sems.at[1]),
    ]
    for copy in copies:
        copy.start()
    channels = charge.shape[0]
    n = jnp.int32(0)
    ends = []
    for wanted in (far[0], -far[0], 0):

        def body(w, n):
            hit = charge[w] == wanted

            @pl.when(hit)
            def _():
                plan[n] = w

            return n + hit.astype(jnp.int32)

        n = lax.fori_loop(0, channels, body, n)
        ends.append(n)
    plan[channels] = ends[0]
    plan[channels + 1] = jnp.maximum(ends[0], ends[1] - ends[0])
    plan[channels + 2] = ends[1]
    plan[channels + 3] = dims[0]
    plan[channels + 4] = dims[1]
    for copy in copies:
        copy.wait()
    inverse[...] = 1.0 / inverse[...]


def bounds(plan):
    channels = plan.shape[0] - 5
    return plan[channels], plan[channels + 1], plan[channels + 2]


def mask_of(plan, rows, width, first=0):
    channels = plan.shape[0] - 5
    a = lax.broadcasted_iota(jnp.int32, (rows, width), 0) + first
    b = lax.broadcasted_iota(jnp.int32, (rows, width), 1)
    return (a < plan[channels + 3]) & (b < plan[channels + 4])


def fold(x):
    return jnp.sum(x.reshape(x.shape[0] // 8, 8, x.shape[1]), axis=0)


def lanes_of(values, lanes):
    lane = lax.broadcasted_iota(jnp.int32, (8, 128), 1)
    out = jnp.zeros((8, 128), F32)
    for value, at in zip(values, lanes):
        whole = jnp.sum(jnp.sum(value, axis=0, keepdims=True), axis=1, keepdims=True)
        out = jnp.where(lane == at, whole, out)
    return out


def first_kernel(
    plan, lb, nb, inv, l_hbm, r_hbm, x_ref, far_ref, near_part, uu_ref,
    t_ref, acc, l_buf, r_buf, sems,
):
    refs = (l_hbm, r_hbm, l_buf, r_buf, sems)
    n_far, head, _ = bounds(plan)

    def start(i, carry):
        for copy in env_copies(i, plan[i], refs):
            copy.start()
        return carry

    lax.fori_loop(0, head, start, 0)
    scaled = (lb[...].astype(F32) * inv[...].astype(F32)).astype(BF16)
    guess = jnp.dot(scaled, nb[...], preferred_element_type=F32)
    guess = jnp.where(mask_of(plan, *guess.shape), guess, 0.0)
    x_ref[...] = guess.astype(BF16)
    uu_ref[...] = lanes_of([fold(guess * guess)], [UU])

    def arrived(i):
        for copy in env_copies(i, plan[i], refs):
            copy.wait()
        return i

    acc[...] = jnp.zeros_like(acc)
    near_part[...] = jnp.zeros_like(near_part)
    apply_channels(plan, 0, n_far, x_ref, t_ref, acc, l_buf, r_buf, arrived)
    far_ref[...] = acc[...].astype(BF16)
    apply_channels(plan, n_far, head, x_ref, t_ref, near_part, l_buf, r_buf, arrived)


def at(red, lane):
    return red[0:1, lane : lane + 1]


def scales_of(reds):
    return [lax.rsqrt(at(reds[0], UU) + EPS)] + [jnp.ones((1, 1), F32)] * (len(reds) - 1)


def solve_step(reds):
    k = len(reds) - 1
    s = scales_of(reds)
    red = reds[k]
    steps = range(k + 1)
    gram = {}
    for i in steps:
        for j in range(i + 1):
            gram[i, j] = gram[j, i] = s[i] * s[j] * at(reds[i], HX + j)
    column = [s[j] * s[k] * at(red, HV + j) for j in steps]
    theta = column[k]
    d = [s[j] * s[k] * (at(red, HA + j) - theta * at(red, HE + j)) for j in steps]
    cc = s[k] * s[k] * (at(red, AA) - 2.0 * theta * at(red, AE) + theta * theta * at(red, EE))
    pp = cc
    for i in steps:
        pp = pp - 2.0 * d[i] * d[i]
        for j in steps:
            pp = pp + d[i] * d[j] * gram[i, j]
    norm = lax.rsqrt(jnp.maximum(pp, 0.0) + EPS)
    return column, norm * s[k], norm * s[k] * theta, [norm * d[j] * s[j] for j in steps]


def following(reds, image, inverse, basis, out):
    _, w_v, w_x, w = solve_step(reds)
    k = len(reds) - 1

    def body(block, carry):
        rows = pl.ds(block * ROWS, ROWS)
        xs = [b[rows, :].astype(F32) for b in basis]
        p = (image[rows, :] * w_v - xs[k] * w_x) * inverse[rows, :]
        for j in range(k + 1):
            p = p - xs[j] * w[j]
        out[rows, :] = p.astype(BF16)
        return carry

    lax.fori_loop(0, out.shape[0] // ROWS, body, 0)


def next_kernel(k, scale, *refs):
    plan, got = refs[:2]
    older = refs[2 : 1 + k]
    basis = refs[1 + k : 1 + 2 * k]
    image, inverse, l_ref, r_ref, x_ref, far_ref, near_part, red_ref, t_ref, acc = refs[1 + 2 * k :]
    n_far, head, _ = bounds(plan)
    red_ref[...] = summed(got, scale)
    reds = [r[...] for r in older] + [red_ref[...]]
    following(reds, image, inverse, basis, x_ref)
    acc[...] = jnp.zeros_like(acc)
    near_part[...] = jnp.zeros_like(near_part)
    apply_channels(plan, 0, n_far, x_ref, t_ref, acc, l_ref, r_ref)
    far_ref[...] = acc[...].astype(BF16)
    apply_channels(plan, n_far, head, x_ref, t_ref, near_part, l_ref, r_ref)


def summed(got, scale):
    return jnp.broadcast_to(jnp.sum(got[...], axis=0) * scale, (8, 128))


def last_kernel(scale, *refs):
    k = MATVECS
    got = refs[0]
    older = refs[1:k]
    basis = refs[k : 2 * k]
    image, inverse, x_hbm, image_hbm, projected, x_buf, sems = refs[2 * k :]
    out = pltpu.make_async_copy(image, image_hbm, sems.at[0])
    out.start()
    reds = [r[...] for r in older] + [summed(got, scale)]
    following(reds, image, inverse, basis, x_buf)
    new = pltpu.make_async_copy(x_buf, x_hbm, sems.at[1])
    new.start()
    row = lax.broadcasted_iota(jnp.int32, (MATVECS, MATVECS), 0)
    col = lax.broadcasted_iota(jnp.int32, (MATVECS, MATVECS), 1)
    table = jnp.zeros((MATVECS, MATVECS), F32)
    for step in range(MATVECS):
        column = solve_step(reds[: step + 1])[0]
        for j in range(step + 1):
            table = jnp.where((row == j) & (col == step), column[j], table)
    projected[...] = table
    new.wait()
    out.wait()


def rest_kernel(k, plan, *refs):
    basis = refs[: k + 1]
    inverse, near_part, l_ref, r_ref, near_ref, stay_ref, dots_ref, t_ref, acc = refs[k + 1 :]
    _, head, split = bounds(plan)
    width = near_ref.shape[1]
    acc[...] = near_part[...]
    apply_channels(plan, head, split, basis[k], t_ref, acc, l_ref, r_ref)
    near_ref[...] = acc[...].astype(BF16)
    stay_ref[...] = jnp.zeros_like(stay_ref)
    apply_channels(plan, split, l_ref.shape[0], basis[k], t_ref, stay_ref, l_ref, r_ref)

    def body(block, sums):
        rows = pl.ds(block * ROWS, ROWS)
        xs = [b[rows, :].astype(F32) for b in basis]
        e = xs[k] * inverse[rows, :]
        new = [x * e for x in xs] + [x * xs[k] for x in xs] + [e * e]
        return tuple(total + fold(x) for total, x in zip(sums, new))

    zero = tuple(jnp.zeros((8, width), F32) for _ in range(2 * k + 3))
    sums = lax.fori_loop(0, near_ref.shape[0] // ROWS, body, zero)
    lanes = [HE + j for j in range(k + 1)] + [HX + j for j in range(k + 1)] + [EE]
    dots_ref[...] = lanes_of(sums, lanes)


def joined_kernel(stay, from_far, out):
    out[...] = stay[...] + from_far[...].astype(F32)


def image_kernel(k, plan, *refs):
    basis = refs[: k + 1]
    stay, from_near, inverse, dots = refs[k + 1 : k + 5]
    rest = refs[k + 5 :]
    if k == 0:
        guess_dots, image, out = rest
    else:
        image, out = rest
    width = stay.shape[1]

    def body(block, sums):
        rows = pl.ds(block * ROWS, ROWS)
        v = stay[rows, :] + from_near[rows, :].astype(F32)
        v = jnp.where(mask_of(plan, ROWS, width, block * ROWS), v, 0.0)
        image[rows, :] = v
        xs = [b[rows, :].astype(F32) for b in basis]
        d = inverse[rows, :]
        a = v * d
        e = xs[k] * d
        new = [x * v for x in xs] + [x * a for x in xs] + [a * a, a * e]
        return tuple(total + fold(x) for total, x in zip(sums, new))

    zero = tuple(jnp.zeros((8, width), F32) for _ in range(2 * k + 4))
    sums = lax.fori_loop(0, stay.shape[0] // ROWS, body, zero)
    lanes = [HV + j for j in range(k + 1)] + [HA + j for j in range(k + 1)] + [AA, AE]
    total = lanes_of(sums, lanes) + dots[...]
    if k == 0:
        total = total + guess_dots[...]
    out[...] = jnp.broadcast_to(total[None, : out.shape[1]], out.shape)


def call(kernel, args, specs, outs, out_specs, scratch, flops, limit):
    return pl.pallas_call(
        kernel,
        out_shape=[jax.ShapeDtypeStruct(*o) for o in outs],
        in_specs=specs,
        out_specs=out_specs,
        scratch_shapes=scratch,
        compiler_params=pltpu.CompilerParams(vmem_limit_bytes=limit * MIB),
        cost_estimate=pl.CostEstimate(
            flops=flops, bytes_accessed=4 * MIB + flops // 512, transcendentals=0
        ),
    )(*args)


def in_hbm(*arrays):
    return [pltpu.with_memory_space_constraint(x, pltpu.HBM) for x in arrays]


def swapped(block, pairs):
    return lax.ppermute(block, "sec", pairs)


def per_device(
    left_env, right_env, left_block, right_block, inv_sv, precond, sector_dims, channel_charge
):
    width = left_block.shape[-1]
    sectors = lax.axis_size("sec")
    segments = lax.axis_size("seg")
    channels = left_env.shape[2]
    scale = 1.0 / (sectors * width * width)
    lenv, renv = left_env[0, 0], right_env[0, 0]
    dims = sector_dims[0, 0]
    odd = lax.rem(lax.axis_index("sec"), 2)
    far = (2 * odd - 1).astype(jnp.int32).reshape(1)
    far_pairs = [(i, i + 1) for i in range(1, sectors - 1, 2)]
    far_pairs += [(j, i) for i, j in far_pairs]
    near_pairs = [(i, i + 1) for i in range(0, sectors, 2)]
    near_pairs += [(j, i) for i, j in near_pairs]
    route = [((i + 1) % segments, i) for i in range(segments)]
    nb, inv = lax.ppermute((right_block[0, 0], inv_sv[0]), "seg", route)

    square = (width, width)
    small = ((8, 128), F32)
    one = 4 * width**3 * channels // 3
    left, inverse, plan = call(
        prepare_kernel,
        (channel_charge, far, dims, *in_hbm(left_block[0, 0], precond[0, 0])),
        [SMEM] * 3 + [HBM] * 2,
        [(square, BF16), (square, F32), ((channels + 5,), jnp.int32)],
        [VMEM, VMEM, SMEM],
        [pltpu.SemaphoreType.DMA((2,))], MIB, 8,
    )
    scratch = [pltpu.VMEM((2, width, width), BF16), pltpu.VMEM(square, F32)]
    buffers = [pltpu.VMEM(lenv.shape, BF16)] * 2 + [pltpu.SemaphoreType.DMA((channels, 2))]
    basis, reds = [], []
    for k in range(MATVECS):
        outs = [(square, BF16), (square, BF16), (square, F32), small]
        if k == 0:
            x, to_far, near_part, guess_dots = call(
                first_kernel,
                (plan, left, nb, inv, *in_hbm(lenv, renv)),
                [SMEM] + [VMEM] * 3 + [HBM] * 2,
                outs, [VMEM] * 4, scratch + buffers, 20 * one, 24,
            )
        else:
            x, to_far, near_part, red = call(
                functools.partial(next_kernel, k, scale),
                (plan, got, *reds, *basis, image, inverse, lenv, renv),
                [SMEM] + [VMEM] * (2 * k + 4),
                outs, [VMEM] * 4, scratch, one, 16,
            )
            reds.append(red)
        basis.append(x)
        from_far = swapped(to_far, far_pairs)
        to_near, stay, dots = call(
            functools.partial(rest_kernel, k),
            (plan, *basis, inverse, near_part, lenv, renv),
            [SMEM] + [VMEM] * (k + 5),
            [(square, BF16), (square, F32), small], [VMEM] * 3,
            scratch, 2 * one, 16,
        )
        from_near = swapped(to_near, near_pairs)
        (stay,) = call(
            joined_kernel, (stay, from_far), [VMEM] * 2, [(square, F32)], [VMEM], [], MIB, 16
        )
        extra = (guess_dots,) if k == 0 else ()
        image, spread = call(
            functools.partial(image_kernel, k),
            (plan, *basis, stay, from_near, inverse, dots, *extra),
            [SMEM] + [VMEM] * (k + 5 + len(extra)),
            [(square, F32), ((sectors, ROW, 128), F32)], [VMEM] * 2,
            [], MIB, 16,
        )
        got = lax.all_to_all(spread, "sec", 0, 0)
    x, image, projected = call(
        functools.partial(last_kernel, scale),
        (got, *reds, *basis, image, inverse),
        [VMEM] * (2 * MATVECS + 2),
        [(square, BF16), (square, F32), ((MATVECS, MATVECS), F32)], [HBM, HBM, VMEM],
        [pltpu.VMEM(square, BF16), pltpu.SemaphoreType.DMA((2,))], MIB, 16,
    )
    return (x[None, None], image[None, None], projected[None])


def solution(mesh):
    in_specs = (
        P("seg", "sec", None, None, None),
        P("seg", "sec", None, None, None),
        P("seg", "sec", None, None),
        P("seg", "sec", None, None),
        P("seg", "sec", None),
        P("seg", "sec", None, None),
        P("seg", "sec", None),
        P(),
    )
    out_specs = (P("seg", "sec", None, None), P("seg", "sec", None, None), P("seg", None, None))
    return jax.shard_map(
        per_device, mesh=mesh, in_specs=in_specs, out_specs=out_specs, check_vma=False
    )
```

```python
import functools

import jax
import jax.numpy as jnp
from jax import lax
from jax.experimental import pallas as pl
from jax.experimental.pallas import tpu as pltpu
from jax.sharding import PartitionSpec as P

MATVECS = 4
EPS = 1e-06
ROWS = 64
ROW = 1
GROUP = 4
MIB = 1 << 20
BF16 = jnp.bfloat16
F32 = jnp.float32
HV, HA, HE, HX, AA, AE, EE, UU = 0, 4, 8, 12, 16, 17, 18, 19

VMEM = pl.BlockSpec(memory_space=pltpu.VMEM)
SMEM = pl.BlockSpec(memory_space=pltpu.SMEM)
HBM = pl.BlockSpec(memory_space=pltpu.HBM)


def env_copies(slot, channel, refs):
    l_hbm, r_hbm, l_buf, r_buf, sems = refs
    return (
        pltpu.make_async_copy(l_hbm.at[channel], l_buf.at[slot], sems.at[slot, 0]),
        pltpu.make_async_copy(r_hbm.at[channel], r_buf.at[slot], sems.at[slot, 1]),
    )


def apply_channels(picked, first, last, x_ref, t_ref, acc, l_ref, r_ref, arrived=None, group_size=GROUP):
    def lefts(i, slot):
        w = picked[i] if arrived is None else arrived(i)
        t_ref[slot] = jnp.dot(l_ref[w], x_ref[...], preferred_element_type=F32).astype(BF16)
        return w

    def term(w, slot):
        return lax.dot_general(
            t_ref[slot], r_ref[w], (((1,), (1,)), ((), ())), preferred_element_type=F32
        )

    def group(start, size):
        ws = [lefts(start + u, u) for u in range(size)]
        parts = [term(w, u) for u, w in enumerate(ws)]
        while len(parts) > 1:
            parts = [x + y for x, y in zip(parts[::2], parts[1::2])]
        acc[...] += parts[0]

    def full(h, carry):
        group(first + group_size * h, group_size)
        return carry

    count = last - first
    lax.fori_loop(0, lax.div(count, group_size), full, 0)
    size = group_size // 2
    while size:
        done = first + lax.div(count, 2 * size) * (2 * size)
        pl.when(lax.rem(lax.div(count, size), 2) == 1)(functools.partial(group, done, size))
        size //= 2


def prepare_kernel(charge, far, dims, lb, precond, lb_out, inverse, plan, sems):
    copies = [
        pltpu.make_async_copy(lb, lb_out, sems.at[0]),
        pltpu.make_async_copy(precond, inverse, sems.at[1]),
    ]
    for copy in copies:
        copy.start()
    channels = charge.shape[0]
    n = jnp.int32(0)
    ends = []
    for wanted in (far[0], -far[0], 0):

        def body(w, n):
            hit = charge[w] == wanted

            @pl.when(hit)
            def _():
                plan[n] = w

            return n + hit.astype(jnp.int32)

        n = lax.fori_loop(0, channels, body, n)
        ends.append(n)
    plan[channels] = ends[0]
    plan[channels + 1] = jnp.maximum(ends[0], ends[1] - ends[0])
    plan[channels + 2] = ends[1]
    plan[channels + 3] = dims[0]
    plan[channels + 4] = dims[1]
    for copy in copies:
        copy.wait()
    inverse[...] = 1.0 / inverse[...]


def bounds(plan):
    channels = plan.shape[0] - 5
    return plan[channels], plan[channels + 1], plan[channels + 2]


def mask_of(plan, rows, width, first=0):
    channels = plan.shape[0] - 5
    a = lax.broadcasted_iota(jnp.int32, (rows, width), 0) + first
    b = lax.broadcasted_iota(jnp.int32, (rows, width), 1)
    return (a < plan[channels + 3]) & (b < plan[channels + 4])


def fold(x):
    return jnp.sum(x.reshape(x.shape[0] // 8, 8, x.shape[1]), axis=0)


def lanes_of(values, lanes):
    lane = lax.broadcasted_iota(jnp.int32, (8, 128), 1)
    out = jnp.zeros((8, 128), F32)
    for value, at in zip(values, lanes):
        whole = jnp.sum(jnp.sum(value, axis=0, keepdims=True), axis=1, keepdims=True)
        out = jnp.where(lane == at, whole, out)
    return out


def first_kernel(
    plan, lb, nb, inv, l_hbm, r_hbm, x_ref, far_ref, near_part, uu_ref,
    t_ref, acc, l_buf, r_buf, sems,
):
    refs = (l_hbm, r_hbm, l_buf, r_buf, sems)
    n_far, head, _ = bounds(plan)

    def start(i, carry):
        for copy in env_copies(i, plan[i], refs):
            copy.start()
        return carry

    lax.fori_loop(0, head, start, 0)
    scaled = (lb[...].astype(F32) * inv[...].astype(F32)).astype(BF16)
    guess = jnp.dot(scaled, nb[...], preferred_element_type=F32)
    guess = jnp.where(mask_of(plan, *guess.shape), guess, 0.0)
    x_ref[...] = guess.astype(BF16)
    uu_ref[...] = lanes_of([fold(guess * guess)], [UU])

    def arrived(i):
        for copy in env_copies(i, plan[i], refs):
            copy.wait()
        return i

    acc[...] = jnp.zeros_like(acc)
    near_part[...] = jnp.zeros_like(near_part)
    apply_channels(plan, 0, n_far, x_ref, t_ref, acc, l_buf, r_buf, arrived)
    far_ref[...] = acc[...].astype(BF16)
    apply_channels(plan, n_far, head, x_ref, t_ref, near_part, l_buf, r_buf, arrived)


def at(red, lane):
    return red[0:1, lane : lane + 1]


def scales_of(reds):
    return [lax.rsqrt(at(reds[0], UU) + EPS)] + [jnp.ones((1, 1), F32)] * (len(reds) - 1)


def solve_step(reds):
    k = len(reds) - 1
    s = scales_of(reds)
    red = reds[k]
    steps = range(k + 1)
    gram = {}
    for i in steps:
        for j in range(i + 1):
            gram[i, j] = gram[j, i] = s[i] * s[j] * at(reds[i], HX + j)
    column = [s[j] * s[k] * at(red, HV + j) for j in steps]
    theta = column[k]
    d = [s[j] * s[k] * (at(red, HA + j) - theta * at(red, HE + j)) for j in steps]
    cc = s[k] * s[k] * (at(red, AA) - 2.0 * theta * at(red, AE) + theta * theta * at(red, EE))
    pp = cc
    for i in steps:
        pp = pp - 2.0 * d[i] * d[i]
        for j in steps:
            pp = pp + d[i] * d[j] * gram[i, j]
    norm = lax.rsqrt(jnp.maximum(pp, 0.0) + EPS)
    return column, norm * s[k], norm * s[k] * theta, [norm * d[j] * s[j] for j in steps]


def following(reds, image, inverse, basis, out):
    _, w_v, w_x, w = solve_step(reds)
    k = len(reds) - 1

    def body(block, carry):
        rows = pl.ds(block * ROWS, ROWS)
        xs = [b[rows, :].astype(F32) for b in basis]
        p = (image[rows, :] * w_v - xs[k] * w_x) * inverse[rows, :]
        for j in range(k + 1):
            p = p - xs[j] * w[j]
        out[rows, :] = p.astype(BF16)
        return carry

    lax.fori_loop(0, out.shape[0] // ROWS, body, 0)


def next_kernel(k, scale, *refs):
    plan, got = refs[:2]
    older = refs[2 : 1 + k]
    basis = refs[1 + k : 1 + 2 * k]
    image, inverse, l_ref, r_ref, x_ref, far_ref, near_part, red_ref, t_ref, acc = refs[1 + 2 * k :]
    n_far, head, _ = bounds(plan)
    red_ref[...] = summed(got, scale)
    reds = [r[...] for r in older] + [red_ref[...]]
    following(reds, image, inverse, basis, x_ref)
    acc[...] = jnp.zeros_like(acc)
    near_part[...] = jnp.zeros_like(near_part)
    apply_channels(plan, 0, n_far, x_ref, t_ref, acc, l_ref, r_ref)
    far_ref[...] = acc[...].astype(BF16)
    apply_channels(plan, n_far, head, x_ref, t_ref, near_part, l_ref, r_ref)


def summed(got, scale):
    return jnp.broadcast_to(jnp.sum(got[...], axis=0) * scale, (8, 128))


def last_kernel(scale, *refs):
    k = MATVECS
    got = refs[0]
    older = refs[1:k]
    basis = refs[k : 2 * k]
    image, inverse, x_hbm, image_hbm, projected, x_buf, sems = refs[2 * k :]
    out = pltpu.make_async_copy(image, image_hbm, sems.at[0])
    out.start()
    reds = [r[...] for r in older] + [summed(got, scale)]
    following(reds, image, inverse, basis, x_buf)
    new = pltpu.make_async_copy(x_buf, x_hbm, sems.at[1])
    new.start()
    row = lax.broadcasted_iota(jnp.int32, (MATVECS, MATVECS), 0)
    col = lax.broadcasted_iota(jnp.int32, (MATVECS, MATVECS), 1)
    table = jnp.zeros((MATVECS, MATVECS), F32)
    for step in range(MATVECS):
        column = solve_step(reds[: step + 1])[0]
        for j in range(step + 1):
            table = jnp.where((row == j) & (col == step), column[j], table)
    projected[...] = table
    new.wait()
    out.wait()


def near_kernel(plan, x, near_part, l_ref, r_ref, near_ref, t_ref, acc):
    _, head, split = bounds(plan)
    acc[...] = near_part[...]
    apply_channels(plan, head, split, x, t_ref, acc, l_ref, r_ref)
    near_ref[...] = acc[...].astype(BF16)


def stay_kernel(k, plan, *refs):
    basis = refs[: k + 1]
    inverse, l_ref, r_ref, stay_ref, dots_ref, t_ref = refs[k + 1 :]
    split = bounds(plan)[2]
    width = stay_ref.shape[1]
    stay_ref[...] = jnp.zeros_like(stay_ref)
    apply_channels(plan, split, l_ref.shape[0], basis[k], t_ref, stay_ref, l_ref, r_ref)

    def body(block, sums):
        rows = pl.ds(block * ROWS, ROWS)
        xs = [b[rows, :].astype(F32) for b in basis]
        e = xs[k] * inverse[rows, :]
        new = [x * e for x in xs] + [x * xs[k] for x in xs] + [e * e]
        return tuple(total + fold(x) for total, x in zip(sums, new))

    zero = tuple(jnp.zeros((8, width), F32) for _ in range(2 * k + 3))
    sums = lax.fori_loop(0, stay_ref.shape[0] // ROWS, body, zero)
    lanes = [HE + j for j in range(k + 1)] + [HX + j for j in range(k + 1)] + [EE]
    dots_ref[...] = lanes_of(sums, lanes)


def joined_kernel(stay, from_far, out):
    out[...] = stay[...] + from_far[...].astype(F32)


def image_kernel(k, plan, *refs):
    basis = refs[: k + 1]
    stay, from_near, inverse, dots = refs[k + 1 : k + 5]
    rest = refs[k + 5 :]
    if k == 0:
        guess_dots, image, out = rest
    else:
        image, out = rest
    width = stay.shape[1]

    def body(block, sums):
        rows = pl.ds(block * ROWS, ROWS)
        v = stay[rows, :] + from_near[rows, :].astype(F32)
        v = jnp.where(mask_of(plan, ROWS, width, block * ROWS), v, 0.0)
        image[rows, :] = v
        xs = [b[rows, :].astype(F32) for b in basis]
        d = inverse[rows, :]
        a = v * d
        e = xs[k] * d
        new = [x * v for x in xs] + [x * a for x in xs] + [a * a, a * e]
        return tuple(total + fold(x) for total, x in zip(sums, new))

    zero = tuple(jnp.zeros((8, width), F32) for _ in range(2 * k + 4))
    sums = lax.fori_loop(0, stay.shape[0] // ROWS, body, zero)
    lanes = [HV + j for j in range(k + 1)] + [HA + j for j in range(k + 1)] + [AA, AE]
    total = lanes_of(sums, lanes) + dots[...]
    if k == 0:
        total = total + guess_dots[...]
    out[...] = jnp.broadcast_to(total[None, : out.shape[1]], out.shape)


def call(kernel, args, specs, outs, out_specs, scratch, flops, limit):
    return pl.pallas_call(
        kernel,
        out_shape=[jax.ShapeDtypeStruct(*o) for o in outs],
        in_specs=specs,
        out_specs=out_specs,
        scratch_shapes=scratch,
        compiler_params=pltpu.CompilerParams(vmem_limit_bytes=limit * MIB),
        cost_estimate=pl.CostEstimate(
            flops=flops, bytes_accessed=4 * MIB + flops // 512, transcendentals=0
        ),
    )(*args)


def in_hbm(*arrays):
    return [pltpu.with_memory_space_constraint(x, pltpu.HBM) for x in arrays]


def swapped(block, pairs):
    return lax.ppermute(block, "sec", pairs)


def per_device(
    left_env, right_env, left_block, right_block, inv_sv, precond, sector_dims, channel_charge
):
    width = left_block.shape[-1]
    sectors = lax.axis_size("sec")
    segments = lax.axis_size("seg")
    channels = left_env.shape[2]
    scale = 1.0 / (sectors * width * width)
    lenv, renv = left_env[0, 0], right_env[0, 0]
    dims = sector_dims[0, 0]
    odd = lax.rem(lax.axis_index("sec"), 2)
    far = (2 * odd - 1).astype(jnp.int32).reshape(1)
    far_pairs = [(i, i + 1) for i in range(1, sectors - 1, 2)]
    far_pairs += [(j, i) for i, j in far_pairs]
    near_pairs = [(i, i + 1) for i in range(0, sectors, 2)]
    near_pairs += [(j, i) for i, j in near_pairs]
    route = [((i + 1) % segments, i) for i in range(segments)]
    nb, inv = lax.ppermute((right_block[0, 0], inv_sv[0]), "seg", route)

    square = (width, width)
    small = ((8, 128), F32)
    one = 4 * width**3 * channels // 3
    left, inverse, plan = call(
        prepare_kernel,
        (channel_charge, far, dims, *in_hbm(left_block[0, 0], precond[0, 0])),
        [SMEM] * 3 + [HBM] * 2,
        [(square, BF16), (square, F32), ((channels + 5,), jnp.int32)],
        [VMEM, VMEM, SMEM],
        [pltpu.SemaphoreType.DMA((2,))], MIB, 8,
    )
    scratch = [pltpu.VMEM((GROUP, width, width), BF16), pltpu.VMEM(square, F32)]
    buffers = [pltpu.VMEM(lenv.shape, BF16)] * 2 + [pltpu.SemaphoreType.DMA((channels, 2))]
    basis, reds = [], []
    for k in range(MATVECS):
        outs = [(square, BF16), (square, BF16), (square, F32), small]
        if k == 0:
            x, to_far, near_part, guess_dots = call(
                first_kernel,
                (plan, left, nb, inv, *in_hbm(lenv, renv)),
                [SMEM] + [VMEM] * 3 + [HBM] * 2,
                outs, [VMEM] * 4, scratch + buffers, 20 * one, 24,
            )
        else:
            x, to_far, near_part, red = call(
                functools.partial(next_kernel, k, scale),
                (plan, got, *reds, *basis, image, inverse, lenv, renv),
                [SMEM] + [VMEM] * (2 * k + 4),
                outs, [VMEM] * 4, scratch, one, 16,
            )
            reds.append(red)
        basis.append(x)
        from_far = swapped(to_far, far_pairs)
        (to_near,) = call(
            near_kernel, (plan, x, near_part, lenv, renv), [SMEM] + [VMEM] * 4,
            [(square, BF16)], [VMEM], scratch, one, 16,
        )
        from_near = swapped(to_near, near_pairs)
        stay, dots = call(
            functools.partial(stay_kernel, k),
            (plan, *basis, inverse, lenv, renv),
            [SMEM] + [VMEM] * (k + 4),
            [(square, F32), small], [VMEM] * 2,
            scratch[:1], one, 16,
        )
        (stay,) = call(
            joined_kernel, (stay, from_far), [VMEM] * 2, [(square, F32)], [VMEM], [], MIB, 16
        )
        extra = (guess_dots,) if k == 0 else ()
        image, spread = call(
            functools.partial(image_kernel, k),
            (plan, *basis, stay, from_near, inverse, dots, *extra),
            [SMEM] + [VMEM] * (k + 5 + len(extra)),
            [(square, F32), ((sectors, ROW, 128), F32)], [VMEM] * 2,
            [], MIB, 16,
        )
        got = lax.all_to_all(spread, "sec", 0, 0)
    x, image, projected = call(
        functools.partial(last_kernel, scale),
        (got, *reds, *basis, image, inverse),
        [VMEM] * (2 * MATVECS + 2),
        [(square, BF16), (square, F32), ((MATVECS, MATVECS), F32)], [HBM, HBM, VMEM],
        [pltpu.VMEM(square, BF16), pltpu.SemaphoreType.DMA((2,))], MIB, 16,
    )
    return (x[None, None], image[None, None], projected[None])


def solution(mesh):
    in_specs = (
        P("seg", "sec", None, None, None),
        P("seg", "sec", None, None, None),
        P("seg", "sec", None, None),
        P("seg", "sec", None, None),
        P("seg", "sec", None),
        P("seg", "sec", None, None),
        P("seg", "sec", None),
        P(),
    )
    out_specs = (P("seg", "sec", None, None), P("seg", "sec", None, None), P("seg", None, None))
    return jax.shard_map(
        per_device, mesh=mesh, in_specs=in_specs, out_specs=out_specs, check_vma=False
    )
```

```python
import functools

import jax
import jax.numpy as jnp
from jax import lax
from jax.experimental import pallas as pl
from jax.experimental.pallas import tpu as pltpu
from jax.sharding import PartitionSpec as P

MATVECS = 4
EPS = 1e-06
ROWS = 64
ROW = 1
MIB = 1 << 20
BF16 = jnp.bfloat16
F32 = jnp.float32
HV, HA, HE, HX, AA, AE, EE, UU = 0, 4, 8, 12, 16, 17, 18, 19

VMEM = pl.BlockSpec(memory_space=pltpu.VMEM)
SMEM = pl.BlockSpec(memory_space=pltpu.SMEM)
HBM = pl.BlockSpec(memory_space=pltpu.HBM)


def env_copies(slot, channel, refs):
    l_hbm, r_hbm, l_buf, r_buf, sems = refs
    return (
        pltpu.make_async_copy(l_hbm.at[channel], l_buf.at[slot], sems.at[slot, 0]),
        pltpu.make_async_copy(r_hbm.at[channel], r_buf.at[slot], sems.at[slot, 1]),
    )


def apply_channels(picked, first, last, x_ref, t_ref, acc, l_ref, r_ref, arrived=None):
    def lefts(i, slot):
        w = picked[i] if arrived is None else arrived(i)
        t_ref[slot] = jnp.dot(l_ref[w], x_ref[...], preferred_element_type=F32).astype(BF16)
        return w

    def term(w, slot):
        return lax.dot_general(
            t_ref[slot], r_ref[w], (((1,), (1,)), ((), ())), preferred_element_type=F32
        )

    def pair(h, carry):
        one = lefts(first + 2 * h, 0)
        two = lefts(first + 2 * h + 1, 1)
        acc[...] += term(one, 0) + term(two, 1)
        return carry

    count = last - first
    lax.fori_loop(0, lax.div(count, 2), pair, 0)

    @pl.when(lax.rem(count, 2) == 1)
    def _():
        acc[...] += term(lefts(last - 1, 0), 0)


def prepare_kernel(charge, far, dims, lb, precond, lb_out, inverse, plan, sems):
    copies = [
        pltpu.make_async_copy(lb, lb_out, sems.at[0]),
        pltpu.make_async_copy(precond, inverse, sems.at[1]),
    ]
    for copy in copies:
        copy.start()
    channels = charge.shape[0]
    n = jnp.int32(0)
    ends = []
    for wanted in (far[0], -far[0], 0):

        def body(w, n):
            hit = charge[w] == wanted

            @pl.when(hit)
            def _():
                plan[n] = w

            return n + hit.astype(jnp.int32)

        n = lax.fori_loop(0, channels, body, n)
        ends.append(n)
    plan[channels] = ends[0]
    plan[channels + 1] = jnp.maximum(ends[0], ends[1] - ends[0])
    plan[channels + 2] = ends[1]
    plan[channels + 3] = dims[0]
    plan[channels + 4] = dims[1]
    for copy in copies:
        copy.wait()
    inverse[...] = 1.0 / inverse[...]


def bounds(plan):
    channels = plan.shape[0] - 5
    return plan[channels], plan[channels + 1], plan[channels + 2]


def mask_of(plan, rows, width, first=0):
    channels = plan.shape[0] - 5
    a = lax.broadcasted_iota(jnp.int32, (rows, width), 0) + first
    b = lax.broadcasted_iota(jnp.int32, (rows, width), 1)
    return (a < plan[channels + 3]) & (b < plan[channels + 4])


def fold(x):
    return jnp.sum(x.reshape(x.shape[0] // 8, 8, x.shape[1]), axis=0)


def lanes_of(values, lanes):
    lane = lax.broadcasted_iota(jnp.int32, (8, 128), 1)
    out = jnp.zeros((8, 128), F32)
    for value, at in zip(values, lanes):
        whole = jnp.sum(jnp.sum(value, axis=0, keepdims=True), axis=1, keepdims=True)
        out = jnp.where(lane == at, whole, out)
    return out


def first_kernel(
    plan, lb, nb, inv, l_hbm, r_hbm, x_ref, far_ref, near_part, uu_ref,
    t_ref, acc, l_buf, r_buf, sems,
):
    refs = (l_hbm, r_hbm, l_buf, r_buf, sems)
    n_far, head, _ = bounds(plan)

    def start(i, carry):
        for copy in env_copies(i, plan[i], refs):
            copy.start()
        return carry

    lax.fori_loop(0, head, start, 0)
    scaled = (lb[...].astype(F32) * inv[...].astype(F32)).astype(BF16)
    guess = jnp.dot(scaled, nb[...], preferred_element_type=F32)
    guess = jnp.where(mask_of(plan, *guess.shape), guess, 0.0)
    x_ref[...] = guess.astype(BF16)
    uu_ref[...] = lanes_of([fold(guess * guess)], [UU])

    def arrived(i):
        for copy in env_copies(i, plan[i], refs):
            copy.wait()
        return i

    acc[...] = jnp.zeros_like(acc)
    near_part[...] = jnp.zeros_like(near_part)
    apply_channels(plan, 0, n_far, x_ref, t_ref, acc, l_buf, r_buf, arrived)
    far_ref[...] = acc[...].astype(BF16)
    apply_channels(plan, n_far, head, x_ref, t_ref, near_part, l_buf, r_buf, arrived)


def at(red, lane):
    return red[0:1, lane : lane + 1]


def scales_of(reds):
    return [lax.rsqrt(at(reds[0], UU) + EPS)] + [jnp.ones((1, 1), F32)] * (len(reds) - 1)


def solve_step(reds):
    k = len(reds) - 1
    s = scales_of(reds)
    red = reds[k]
    steps = range(k + 1)
    gram = {}
    for i in steps:
        for j in range(i + 1):
            gram[i, j] = gram[j, i] = s[i] * s[j] * at(reds[i], HX + j)
    column = [s[j] * s[k] * at(red, HV + j) for j in steps]
    theta = column[k]
    d = [s[j] * s[k] * (at(red, HA + j) - theta * at(red, HE + j)) for j in steps]
    cc = s[k] * s[k] * (at(red, AA) - 2.0 * theta * at(red, AE) + theta * theta * at(red, EE))
    pp = cc
    for i in steps:
        pp = pp - 2.0 * d[i] * d[i]
        for j in steps:
            pp = pp + d[i] * d[j] * gram[i, j]
    norm = lax.rsqrt(jnp.maximum(pp, 0.0) + EPS)
    return column, norm * s[k], norm * s[k] * theta, [norm * d[j] * s[j] for j in steps]


def following(reds, image, inverse, basis, out):
    _, w_v, w_x, w = solve_step(reds)
    k = len(reds) - 1

    def body(block, carry):
        rows = pl.ds(block * ROWS, ROWS)
        xs = [b[rows, :].astype(F32) for b in basis]
        p = (image[rows, :] * w_v - xs[k] * w_x) * inverse[rows, :]
        for j in range(k + 1):
            p = p - xs[j] * w[j]
        out[rows, :] = p.astype(BF16)
        return carry

    lax.fori_loop(0, out.shape[0] // ROWS, body, 0)


def next_kernel(k, scale, *refs):
    plan, got = refs[:2]
    older = refs[2 : 1 + k]
    basis = refs[1 + k : 1 + 2 * k]
    image, inverse, l_ref, r_ref, x_ref, far_ref, near_part, red_ref, t_ref, acc = refs[1 + 2 * k :]
    n_far, head, _ = bounds(plan)
    red_ref[...] = summed(got, scale)
    reds = [r[...] for r in older] + [red_ref[...]]
    following(reds, image, inverse, basis, x_ref)
    acc[...] = jnp.zeros_like(acc)
    near_part[...] = jnp.zeros_like(near_part)
    apply_channels(plan, 0, n_far, x_ref, t_ref, acc, l_ref, r_ref)
    far_ref[...] = acc[...].astype(BF16)
    apply_channels(plan, n_far, head, x_ref, t_ref, near_part, l_ref, r_ref)


def summed(got, scale):
    return jnp.broadcast_to(jnp.sum(got[...], axis=0) * scale, (8, 128))


def last_kernel(scale, *refs):
    k = MATVECS
    got = refs[0]
    older = refs[1:k]
    basis = refs[k : 2 * k]
    image, inverse, x_hbm, image_hbm, projected, x_buf, sems = refs[2 * k :]
    out = pltpu.make_async_copy(image, image_hbm, sems.at[0])
    out.start()
    reds = [r[...] for r in older] + [summed(got, scale)]
    following(reds, image, inverse, basis, x_buf)
    new = pltpu.make_async_copy(x_buf, x_hbm, sems.at[1])
    new.start()
    row = lax.broadcasted_iota(jnp.int32, (MATVECS, MATVECS), 0)
    col = lax.broadcasted_iota(jnp.int32, (MATVECS, MATVECS), 1)
    table = jnp.zeros((MATVECS, MATVECS), F32)
    for step in range(MATVECS):
        column = solve_step(reds[: step + 1])[0]
        for j in range(step + 1):
            table = jnp.where((row == j) & (col == step), column[j], table)
    projected[...] = table
    new.wait()
    out.wait()


def near_kernel(plan, x, near_part, l_ref, r_ref, near_ref, t_ref, acc):
    _, head, split = bounds(plan)
    acc[...] = near_part[...]
    apply_channels(plan, head, split, x, t_ref, acc, l_ref, r_ref)
    near_ref[...] = acc[...].astype(BF16)


def stay_kernel(k, plan, *refs):
    basis = refs[: k + 1]
    inverse, l_ref, r_ref, stay_ref, dots_ref, t_ref = refs[k + 1 :]
    split = bounds(plan)[2]
    width = stay_ref.shape[1]
    stay_ref[...] = jnp.zeros_like(stay_ref)
    apply_channels(plan, split, l_ref.shape[0], basis[k], t_ref, stay_ref, l_ref, r_ref)

    def body(block, sums):
        rows = pl.ds(block * ROWS, ROWS)
        xs = [b[rows, :].astype(F32) for b in basis]
        e = xs[k] * inverse[rows, :]
        new = [x * e for x in xs] + [x * xs[k] for x in xs] + [e * e]
        return tuple(total + fold(x) for total, x in zip(sums, new))

    zero = tuple(jnp.zeros((8, width), F32) for _ in range(2 * k + 3))
    sums = lax.fori_loop(0, stay_ref.shape[0] // ROWS, body, zero)
    lanes = [HE + j for j in range(k + 1)] + [HX + j for j in range(k + 1)] + [EE]
    dots_ref[...] = lanes_of(sums, lanes)


def joined_kernel(stay, from_far, out):
    out[...] = stay[...] + from_far[...].astype(F32)


def image_kernel(k, plan, *refs):
    basis = refs[: k + 1]
    stay, from_near, inverse, dots = refs[k + 1 : k + 5]
    rest = refs[k + 5 :]
    if k == 0:
        guess_dots, image, out = rest
    else:
        image, out = rest
    width = stay.shape[1]

    def body(block, sums):
        rows = pl.ds(block * ROWS, ROWS)
        v = stay[rows, :] + from_near[rows, :].astype(F32)
        v = jnp.where(mask_of(plan, ROWS, width, block * ROWS), v, 0.0)
        image[rows, :] = v
        xs = [b[rows, :].astype(F32) for b in basis]
        d = inverse[rows, :]
        a = v * d
        e = xs[k] * d
        new = [x * v for x in xs] + [x * a for x in xs] + [a * a, a * e]
        return tuple(total + fold(x) for total, x in zip(sums, new))

    zero = tuple(jnp.zeros((8, width), F32) for _ in range(2 * k + 4))
    sums = lax.fori_loop(0, stay.shape[0] // ROWS, body, zero)
    lanes = [HV + j for j in range(k + 1)] + [HA + j for j in range(k + 1)] + [AA, AE]
    total = lanes_of(sums, lanes) + dots[...]
    if k == 0:
        total = total + guess_dots[...]
    out[...] = jnp.broadcast_to(total[None, : out.shape[1]], out.shape)


def call(kernel, args, specs, outs, out_specs, scratch, flops, limit):
    return pl.pallas_call(
        kernel,
        out_shape=[jax.ShapeDtypeStruct(*o) for o in outs],
        in_specs=specs,
        out_specs=out_specs,
        scratch_shapes=scratch,
        compiler_params=pltpu.CompilerParams(vmem_limit_bytes=limit * MIB),
        cost_estimate=pl.CostEstimate(
            flops=flops, bytes_accessed=4 * MIB + flops // 512, transcendentals=0
        ),
    )(*args)


def in_hbm(*arrays):
    return [pltpu.with_memory_space_constraint(x, pltpu.HBM) for x in arrays]


def swapped(block, pairs):
    return lax.ppermute(block, "sec", pairs)


def per_device(
    left_env, right_env, left_block, right_block, inv_sv, precond, sector_dims, channel_charge
):
    width = left_block.shape[-1]
    sectors = lax.axis_size("sec")
    segments = lax.axis_size("seg")
    channels = left_env.shape[2]
    scale = 1.0 / (sectors * width * width)
    lenv, renv = left_env[0, 0], right_env[0, 0]
    dims = sector_dims[0, 0]
    odd = lax.rem(lax.axis_index("sec"), 2)
    far = (2 * odd - 1).astype(jnp.int32).reshape(1)
    far_pairs = [(i, i + 1) for i in range(1, sectors - 1, 2)]
    far_pairs += [(j, i) for i, j in far_pairs]
    near_pairs = [(i, i + 1) for i in range(0, sectors, 2)]
    near_pairs += [(j, i) for i, j in near_pairs]
    route = [((i + 1) % segments, i) for i in range(segments)]
    nb, inv = lax.ppermute((right_block[0, 0], inv_sv[0]), "seg", route)

    square = (width, width)
    small = ((8, 128), F32)
    one = 4 * width**3 * channels // 3
    left, inverse, plan = call(
        prepare_kernel,
        (channel_charge, far, dims, *in_hbm(left_block[0, 0], precond[0, 0])),
        [SMEM] * 3 + [HBM] * 2,
        [(square, BF16), (square, F32), ((channels + 5,), jnp.int32)],
        [VMEM, VMEM, SMEM],
        [pltpu.SemaphoreType.DMA((2,))], MIB, 8,
    )
    scratch = [pltpu.VMEM((2, width, width), BF16), pltpu.VMEM(square, F32)]
    buffers = [pltpu.VMEM(lenv.shape, BF16)] * 2 + [pltpu.SemaphoreType.DMA((channels, 2))]
    basis, reds = [], []
    for k in range(MATVECS):
        outs = [(square, BF16), (square, BF16), (square, F32), small]
        if k == 0:
            x, to_far, near_part, guess_dots = call(
                first_kernel,
                (plan, left, nb, inv, *in_hbm(lenv, renv)),
                [SMEM] + [VMEM] * 3 + [HBM] * 2,
                outs, [VMEM] * 4, scratch + buffers, 20 * one, 24,
            )
        else:
            x, to_far, near_part, red = call(
                functools.partial(next_kernel, k, scale),
                (plan, got, *reds, *basis, image, inverse, lenv, renv),
                [SMEM] + [VMEM] * (2 * k + 4),
                outs, [VMEM] * 4, scratch, one, 16,
            )
            reds.append(red)
        basis.append(x)
        from_far = swapped(to_far, far_pairs)
        (to_near,) = call(
            near_kernel, (plan, x, near_part, lenv, renv), [SMEM] + [VMEM] * 4,
            [(square, BF16)], [VMEM], scratch, one, 16,
        )
        from_near = swapped(to_near, near_pairs)
        stay, dots = call(
            functools.partial(stay_kernel, k),
            (plan, *basis, inverse, lenv, renv),
            [SMEM] + [VMEM] * (k + 4),
            [(square, F32), small], [VMEM] * 2,
            scratch[:1], one, 16,
        )
        (stay,) = call(
            joined_kernel, (stay, from_far), [VMEM] * 2, [(square, F32)], [VMEM], [], MIB, 16
        )
        extra = (guess_dots,) if k == 0 else ()
        image, spread = call(
            functools.partial(image_kernel, k),
            (plan, *basis, stay, from_near, inverse, dots, *extra),
            [SMEM] + [VMEM] * (k + 5 + len(extra)),
            [(square, F32), ((sectors, ROW, 128), F32)], [VMEM] * 2,
            [], MIB, 16,
        )
        got = lax.all_to_all(spread, "sec", 0, 0)
    x, image, projected = call(
        functools.partial(last_kernel, scale),
        (got, *reds, *basis, image, inverse),
        [VMEM] * (2 * MATVECS + 2),
        [(square, BF16), (square, F32), ((MATVECS, MATVECS), F32)], [HBM, HBM, VMEM],
        [pltpu.VMEM(square, BF16), pltpu.SemaphoreType.DMA((2,))], MIB, 16,
    )
    return (x[None, None], image[None, None], projected[None])


def solution(mesh):
    in_specs = (
        P("seg", "sec", None, None, None),
        P("seg", "sec", None, None, None),
        P("seg", "sec", None, None),
        P("seg", "sec", None, None),
        P("seg", "sec", None),
        P("seg", "sec", None, None),
        P("seg", "sec", None),
        P(),
    )
    out_specs = (P("seg", "sec", None, None), P("seg", "sec", None, None), P("seg", None, None))
    return jax.shard_map(
        per_device, mesh=mesh, in_specs=in_specs, out_specs=out_specs, check_vma=False
    )
```

```python
import functools

import jax
import jax.numpy as jnp
from jax import lax
from jax.experimental import pallas as pl
from jax.experimental.pallas import tpu as pltpu
from jax.sharding import PartitionSpec as P

MATVECS = 4
EPS = 1e-06
ROWS = 64
ROW = 1
GROUP = 4
MIB = 1 << 20
BF16 = jnp.bfloat16
F32 = jnp.float32
HV, HA, HE, HX, AA, AE, EE, UU = 0, 4, 8, 12, 16, 17, 18, 19

VMEM = pl.BlockSpec(memory_space=pltpu.VMEM)
SMEM = pl.BlockSpec(memory_space=pltpu.SMEM)
HBM = pl.BlockSpec(memory_space=pltpu.HBM)


def env_copies(slot, channel, refs):
    l_hbm, r_hbm, l_buf, r_buf, sems = refs
    return (
        pltpu.make_async_copy(l_hbm.at[channel], l_buf.at[slot], sems.at[slot, 0]),
        pltpu.make_async_copy(r_hbm.at[channel], r_buf.at[slot], sems.at[slot, 1]),
    )


def apply_channels(picked, first, last, x_ref, t_ref, acc, l_ref, r_ref, arrived=None):
    def lefts(i, slot):
        w = picked[i] if arrived is None else arrived(i)
        t_ref[slot] = jnp.dot(l_ref[w], x_ref[...], preferred_element_type=F32).astype(BF16)
        return w

    def term(w, slot):
        return lax.dot_general(
            t_ref[slot], r_ref[w], (((1,), (1,)), ((), ())), preferred_element_type=F32
        )

    def pair(h, carry):
        one = lefts(first + 2 * h, 0)
        two = lefts(first + 2 * h + 1, 1)
        acc[...] += term(one, 0) + term(two, 1)
        return carry

    count = last - first
    lax.fori_loop(0, lax.div(count, 2), pair, 0)

    @pl.when(lax.rem(count, 2) == 1)
    def _():
        acc[...] += term(lefts(last - 1, 0), 0)


def apply_head(plan, x_ref, t_ref, sums, l_ref, r_ref, arrived=None):
    n_far, head, _ = bounds(plan)
    sums[...] = jnp.zeros_like(sums)

    def group(start, size):
        ws = []
        for u in range(size):
            w = plan[start + u] if arrived is None else arrived(start + u)
            t_ref[u] = jnp.dot(l_ref[w], x_ref[...], preferred_element_type=F32).astype(BF16)
            ws.append(w)
        for u, w in enumerate(ws):
            side = (start + u >= n_far).astype(jnp.int32)
            sums[side] += lax.dot_general(
                t_ref[u], r_ref[w], (((1,), (1,)), ((), ())), preferred_element_type=F32
            )

    def full(h, carry):
        group(GROUP * h, GROUP)
        return carry

    lax.fori_loop(0, lax.div(head, GROUP), full, 0)
    size = GROUP // 2
    while size:
        done = lax.div(head, 2 * size) * (2 * size)
        pl.when(lax.rem(lax.div(head, size), 2) == 1)(functools.partial(group, done, size))
        size //= 2


def prepare_kernel(charge, far, dims, lb, precond, lb_out, inverse, plan, sems):
    copies = [
        pltpu.make_async_copy(lb, lb_out, sems.at[0]),
        pltpu.make_async_copy(precond, inverse, sems.at[1]),
    ]
    for copy in copies:
        copy.start()
    channels = charge.shape[0]
    n = jnp.int32(0)
    ends = []
    for wanted in (far[0], -far[0], 0):

        def body(w, n):
            hit = charge[w] == wanted

            @pl.when(hit)
            def _():
                plan[n] = w

            return n + hit.astype(jnp.int32)

        n = lax.fori_loop(0, channels, body, n)
        ends.append(n)
    plan[channels] = ends[0]
    plan[channels + 1] = jnp.maximum(ends[0], ends[1] - ends[0])
    plan[channels + 2] = ends[1]
    plan[channels + 3] = dims[0]
    plan[channels + 4] = dims[1]
    for copy in copies:
        copy.wait()
    inverse[...] = 1.0 / inverse[...]


def bounds(plan):
    channels = plan.shape[0] - 5
    return plan[channels], plan[channels + 1], plan[channels + 2]


def mask_of(plan, rows, width, first=0):
    channels = plan.shape[0] - 5
    a = lax.broadcasted_iota(jnp.int32, (rows, width), 0) + first
    b = lax.broadcasted_iota(jnp.int32, (rows, width), 1)
    return (a < plan[channels + 3]) & (b < plan[channels + 4])


def fold(x):
    return jnp.sum(x.reshape(x.shape[0] // 8, 8, x.shape[1]), axis=0)


def lanes_of(values, lanes):
    lane = lax.broadcasted_iota(jnp.int32, (8, 128), 1)
    out = jnp.zeros((8, 128), F32)
    for value, at in zip(values, lanes):
        whole = jnp.sum(jnp.sum(value, axis=0, keepdims=True), axis=1, keepdims=True)
        out = jnp.where(lane == at, whole, out)
    return out


def first_kernel(
    plan, lb, nb, inv, l_hbm, r_hbm, x_ref, far_ref, head_sums, uu_ref,
    t_ref, l_buf, r_buf, sems,
):
    refs = (l_hbm, r_hbm, l_buf, r_buf, sems)
    head = bounds(plan)[1]

    def start(i, carry):
        for copy in env_copies(i, plan[i], refs):
            copy.start()
        return carry

    lax.fori_loop(0, head, start, 0)
    scaled = (lb[...].astype(F32) * inv[...].astype(F32)).astype(BF16)
    guess = jnp.dot(scaled, nb[...], preferred_element_type=F32)
    guess = jnp.where(mask_of(plan, *guess.shape), guess, 0.0)
    x_ref[...] = guess.astype(BF16)
    uu_ref[...] = lanes_of([fold(guess * guess)], [UU])

    def arrived(i):
        for copy in env_copies(i, plan[i], refs):
            copy.wait()
        return i

    apply_head(plan, x_ref, t_ref, head_sums, l_buf, r_buf, arrived)
    far_ref[...] = head_sums[0].astype(BF16)


def at(red, lane):
    return red[0:1, lane : lane + 1]


def scales_of(reds):
    return [lax.rsqrt(at(reds[0], UU) + EPS)] + [jnp.ones((1, 1), F32)] * (len(reds) - 1)


def solve_step(reds):
    k = len(reds) - 1
    s = scales_of(reds)
    red = reds[k]
    steps = range(k + 1)
    gram = {}
    for i in steps:
        for j in range(i + 1):
            gram[i, j] = gram[j, i] = s[i] * s[j] * at(reds[i], HX + j)
    column = [s[j] * s[k] * at(red, HV + j) for j in steps]
    theta = column[k]
    d = [s[j] * s[k] * (at(red, HA + j) - theta * at(red, HE + j)) for j in steps]
    cc = s[k] * s[k] * (at(red, AA) - 2.0 * theta * at(red, AE) + theta * theta * at(red, EE))
    pp = cc
    for i in steps:
        pp = pp - 2.0 * d[i] * d[i]
        for j in steps:
            pp = pp + d[i] * d[j] * gram[i, j]
    norm = lax.rsqrt(jnp.maximum(pp, 0.0) + EPS)
    return column, norm * s[k], norm * s[k] * theta, [norm * d[j] * s[j] for j in steps]


def following(reds, image, inverse, basis, out):
    _, w_v, w_x, w = solve_step(reds)
    k = len(reds) - 1

    def body(block, carry):
        rows = pl.ds(block * ROWS, ROWS)
        xs = [b[rows, :].astype(F32) for b in basis]
        p = (image[rows, :] * w_v - xs[k] * w_x) * inverse[rows, :]
        for j in range(k + 1):
            p = p - xs[j] * w[j]
        out[rows, :] = p.astype(BF16)
        return carry

    lax.fori_loop(0, out.shape[0] // ROWS, body, 0)


def next_kernel(k, scale, *refs):
    plan, got = refs[:2]
    older = refs[2 : 1 + k]
    basis = refs[1 + k : 1 + 2 * k]
    image, inverse, l_ref, r_ref, x_ref, far_ref, head_sums, red_ref, t_ref = refs[1 + 2 * k :]
    red_ref[...] = summed(got, scale)
    reds = [r[...] for r in older] + [red_ref[...]]
    following(reds, image, inverse, basis, x_ref)
    apply_head(plan, x_ref, t_ref, head_sums, l_ref, r_ref)
    far_ref[...] = head_sums[0].astype(BF16)


def summed(got, scale):
    return jnp.broadcast_to(jnp.sum(got[...], axis=0) * scale, (8, 128))


def last_kernel(scale, *refs):
    k = MATVECS
    got = refs[0]
    older = refs[1:k]
    basis = refs[k : 2 * k]
    image, inverse, x_hbm, image_hbm, projected, x_buf, sems = refs[2 * k :]
    out = pltpu.make_async_copy(image, image_hbm, sems.at[0])
    out.start()
    reds = [r[...] for r in older] + [summed(got, scale)]
    following(reds, image, inverse, basis, x_buf)
    new = pltpu.make_async_copy(x_buf, x_hbm, sems.at[1])
    new.start()
    row = lax.broadcasted_iota(jnp.int32, (MATVECS, MATVECS), 0)
    col = lax.broadcasted_iota(jnp.int32, (MATVECS, MATVECS), 1)
    table = jnp.zeros((MATVECS, MATVECS), F32)
    for step in range(MATVECS):
        column = solve_step(reds[: step + 1])[0]
        for j in range(step + 1):
            table = jnp.where((row == j) & (col == step), column[j], table)
    projected[...] = table
    new.wait()
    out.wait()


def near_kernel(plan, x, head_sums, l_ref, r_ref, near_ref, t_ref, acc):
    _, head, split = bounds(plan)
    acc[...] = head_sums[1]
    apply_channels(plan, head, split, x, t_ref, acc, l_ref, r_ref)
    near_ref[...] = acc[...].astype(BF16)


def stay_kernel(k, plan, *refs):
    basis = refs[: k + 1]
    inverse, l_ref, r_ref, stay_ref, dots_ref, t_ref = refs[k + 1 :]
    split = bounds(plan)[2]
    width = stay_ref.shape[1]
    stay_ref[...] = jnp.zeros_like(stay_ref)
    apply_channels(plan, split, l_ref.shape[0], basis[k], t_ref, stay_ref, l_ref, r_ref)

    def body(block, sums):
        rows = pl.ds(block * ROWS, ROWS)
        xs = [b[rows, :].astype(F32) for b in basis]
        e = xs[k] * inverse[rows, :]
        new = [x * e for x in xs] + [x * xs[k] for x in xs] + [e * e]
        return tuple(total + fold(x) for total, x in zip(sums, new))

    zero = tuple(jnp.zeros((8, width), F32) for _ in range(2 * k + 3))
    sums = lax.fori_loop(0, stay_ref.shape[0] // ROWS, body, zero)
    lanes = [HE + j for j in range(k + 1)] + [HX + j for j in range(k + 1)] + [EE]
    dots_ref[...] = lanes_of(sums, lanes)


def joined_kernel(stay, from_far, out):
    out[...] = stay[...] + from_far[...].astype(F32)


def image_kernel(k, plan, *refs):
    basis = refs[: k + 1]
    stay, from_near, inverse, dots = refs[k + 1 : k + 5]
    rest = refs[k + 5 :]
    if k == 0:
        guess_dots, image, out = rest
    else:
        image, out = rest
    width = stay.shape[1]

    def body(block, sums):
        rows = pl.ds(block * ROWS, ROWS)
        v = stay[rows, :] + from_near[rows, :].astype(F32)
        v = jnp.where(mask_of(plan, ROWS, width, block * ROWS), v, 0.0)
        image[rows, :] = v
        xs = [b[rows, :].astype(F32) for b in basis]
        d = inverse[rows, :]
        a = v * d
        e = xs[k] * d
        new = [x * v for x in xs] + [x * a for x in xs] + [a * a, a * e]
        return tuple(total + fold(x) for total, x in zip(sums, new))

    zero = tuple(jnp.zeros((8, width), F32) for _ in range(2 * k + 4))
    sums = lax.fori_loop(0, stay.shape[0] // ROWS, body, zero)
    lanes = [HV + j for j in range(k + 1)] + [HA + j for j in range(k + 1)] + [AA, AE]
    total = lanes_of(sums, lanes) + dots[...]
    if k == 0:
        total = total + guess_dots[...]
    out[...] = jnp.broadcast_to(total[None, : out.shape[1]], out.shape)


def call(kernel, args, specs, outs, out_specs, scratch, flops, limit):
    return pl.pallas_call(
        kernel,
        out_shape=[jax.ShapeDtypeStruct(*o) for o in outs],
        in_specs=specs,
        out_specs=out_specs,
        scratch_shapes=scratch,
        compiler_params=pltpu.CompilerParams(vmem_limit_bytes=limit * MIB),
        cost_estimate=pl.CostEstimate(
            flops=flops, bytes_accessed=4 * MIB + flops // 512, transcendentals=0
        ),
    )(*args)


def in_hbm(*arrays):
    return [pltpu.with_memory_space_constraint(x, pltpu.HBM) for x in arrays]


def swapped(block, pairs):
    return lax.ppermute(block, "sec", pairs)


def per_device(
    left_env, right_env, left_block, right_block, inv_sv, precond, sector_dims, channel_charge
):
    width = left_block.shape[-1]
    sectors = lax.axis_size("sec")
    segments = lax.axis_size("seg")
    channels = left_env.shape[2]
    scale = 1.0 / (sectors * width * width)
    lenv, renv = left_env[0, 0], right_env[0, 0]
    dims = sector_dims[0, 0]
    odd = lax.rem(lax.axis_index("sec"), 2)
    far = (2 * odd - 1).astype(jnp.int32).reshape(1)
    far_pairs = [(i, i + 1) for i in range(1, sectors - 1, 2)]
    far_pairs += [(j, i) for i, j in far_pairs]
    near_pairs = [(i, i + 1) for i in range(0, sectors, 2)]
    near_pairs += [(j, i) for i, j in near_pairs]
    route = [((i + 1) % segments, i) for i in range(segments)]
    nb, inv = lax.ppermute((right_block[0, 0], inv_sv[0]), "seg", route)

    square = (width, width)
    small = ((8, 128), F32)
    one = 4 * width**3 * channels // 3
    left, inverse, plan = call(
        prepare_kernel,
        (channel_charge, far, dims, *in_hbm(left_block[0, 0], precond[0, 0])),
        [SMEM] * 3 + [HBM] * 2,
        [(square, BF16), (square, F32), ((channels + 5,), jnp.int32)],
        [VMEM, VMEM, SMEM],
        [pltpu.SemaphoreType.DMA((2,))], MIB, 8,
    )
    scratch = [pltpu.VMEM((2, width, width), BF16), pltpu.VMEM(square, F32)]
    head_scratch = [pltpu.VMEM((GROUP, width, width), BF16)]
    buffers = [pltpu.VMEM(lenv.shape, BF16)] * 2 + [pltpu.SemaphoreType.DMA((channels, 2))]
    basis, reds = [], []
    for k in range(MATVECS):
        outs = [(square, BF16), (square, BF16), ((2, width, width), F32), small]
        if k == 0:
            x, to_far, head_sums, guess_dots = call(
                first_kernel,
                (plan, left, nb, inv, *in_hbm(lenv, renv)),
                [SMEM] + [VMEM] * 3 + [HBM] * 2,
                outs, [VMEM] * 4, head_scratch + buffers, 20 * one, 24,
            )
        else:
            x, to_far, head_sums, red = call(
                functools.partial(next_kernel, k, scale),
                (plan, got, *reds, *basis, image, inverse, lenv, renv),
                [SMEM] + [VMEM] * (2 * k + 4),
                outs, [VMEM] * 4, head_scratch, one, 16,
            )
            reds.append(red)
        basis.append(x)
        from_far = swapped(to_far, far_pairs)
        (to_near,) = call(
            near_kernel, (plan, x, head_sums, lenv, renv), [SMEM] + [VMEM] * 4,
            [(square, BF16)], [VMEM], scratch, one, 16,
        )
        from_near = swapped(to_near, near_pairs)
        stay, dots = call(
            functools.partial(stay_kernel, k),
            (plan, *basis, inverse, lenv, renv),
            [SMEM] + [VMEM] * (k + 4),
            [(square, F32), small], [VMEM] * 2,
            scratch[:1], one, 16,
        )
        (stay,) = call(
            joined_kernel, (stay, from_far), [VMEM] * 2, [(square, F32)], [VMEM], [], MIB, 16
        )
        extra = (guess_dots,) if k == 0 else ()
        image, spread = call(
            functools.partial(image_kernel, k),
            (plan, *basis, stay, from_near, inverse, dots, *extra),
            [SMEM] + [VMEM] * (k + 5 + len(extra)),
            [(square, F32), ((sectors, ROW, 128), F32)], [VMEM] * 2,
            [], MIB, 16,
        )
        got = lax.all_to_all(spread, "sec", 0, 0)
    x, image, projected = call(
        functools.partial(last_kernel, scale),
        (got, *reds, *basis, image, inverse),
        [VMEM] * (2 * MATVECS + 2),
        [(square, BF16), (square, F32), ((MATVECS, MATVECS), F32)], [HBM, HBM, VMEM],
        [pltpu.VMEM(square, BF16), pltpu.SemaphoreType.DMA((2,))], MIB, 16,
    )
    return (x[None, None], image[None, None], projected[None])


def solution(mesh):
    in_specs = (
        P("seg", "sec", None, None, None),
        P("seg", "sec", None, None, None),
        P("seg", "sec", None, None),
        P("seg", "sec", None, None),
        P("seg", "sec", None),
        P("seg", "sec", None, None),
        P("seg", "sec", None),
        P(),
    )
    out_specs = (P("seg", "sec", None, None), P("seg", "sec", None, None), P("seg", None, None))
    return jax.shard_map(
        per_device, mesh=mesh, in_specs=in_specs, out_specs=out_specs, check_vma=False
    )
```

```python
import functools

import jax
import jax.numpy as jnp
from jax import lax
from jax.experimental import pallas as pl
from jax.experimental.pallas import tpu as pltpu
from jax.sharding import PartitionSpec as P

MATVECS = 4
EPS = 1e-06
ROWS = 32
ROW = 1
GROUP = 4
MIB = 1 << 20
BF16 = jnp.bfloat16
F32 = jnp.float32
HV, HA, HE, HX, AA, AE, EE, UU = 0, 4, 8, 12, 16, 17, 18, 19

VMEM = pl.BlockSpec(memory_space=pltpu.VMEM)
SMEM = pl.BlockSpec(memory_space=pltpu.SMEM)
HBM = pl.BlockSpec(memory_space=pltpu.HBM)


def env_copies(slot, channel, refs):
    l_hbm, r_hbm, l_buf, r_buf, sems = refs
    return (
        pltpu.make_async_copy(l_hbm.at[channel], l_buf.at[slot], sems.at[slot, 0]),
        pltpu.make_async_copy(r_hbm.at[channel], r_buf.at[slot], sems.at[slot, 1]),
    )


def apply_channels(picked, first, last, x_ref, t_ref, acc, l_ref, r_ref, arrived=None):
    def lefts(i, slot):
        w = picked[i] if arrived is None else arrived(i)
        t_ref[slot] = jnp.dot(l_ref[w], x_ref[...], preferred_element_type=F32).astype(BF16)
        return w

    def term(w, slot):
        return lax.dot_general(
            t_ref[slot], r_ref[w], (((1,), (1,)), ((), ())), preferred_element_type=F32
        )

    def pair(h, carry):
        one = lefts(first + 2 * h, 0)
        two = lefts(first + 2 * h + 1, 1)
        acc[...] += term(one, 0) + term(two, 1)
        return carry

    count = last - first
    lax.fori_loop(0, lax.div(count, 2), pair, 0)

    @pl.when(lax.rem(count, 2) == 1)
    def _():
        acc[...] += term(lefts(last - 1, 0), 0)


def apply_head(plan, x_ref, t_ref, sums, l_ref, r_ref, arrived=None):
    n_far, head, _ = bounds(plan)
    sums[...] = jnp.zeros_like(sums)

    def group(start, size):
        ws = []
        for u in range(size):
            w = plan[start + u] if arrived is None else arrived(start + u)
            t_ref[u] = jnp.dot(l_ref[w], x_ref[...], preferred_element_type=F32).astype(BF16)
            ws.append(w)
        for u, w in enumerate(ws):
            side = (start + u >= n_far).astype(jnp.int32)
            sums[side] += lax.dot_general(
                t_ref[u], r_ref[w], (((1,), (1,)), ((), ())), preferred_element_type=F32
            )

    def full(h, carry):
        group(GROUP * h, GROUP)
        return carry

    lax.fori_loop(0, lax.div(head, GROUP), full, 0)
    size = GROUP // 2
    while size:
        done = lax.div(head, 2 * size) * (2 * size)
        pl.when(lax.rem(lax.div(head, size), 2) == 1)(functools.partial(group, done, size))
        size //= 2


def prepare_kernel(charge, far, dims, lb, precond, lb_out, inverse, plan, sems):
    copies = [
        pltpu.make_async_copy(lb, lb_out, sems.at[0]),
        pltpu.make_async_copy(precond, inverse, sems.at[1]),
    ]
    for copy in copies:
        copy.start()
    channels = charge.shape[0]
    n = jnp.int32(0)
    ends = []
    for wanted in (far[0], -far[0], 0):

        def body(w, n):
            hit = charge[w] == wanted

            @pl.when(hit)
            def _():
                plan[n] = w

            return n + hit.astype(jnp.int32)

        n = lax.fori_loop(0, channels, body, n)
        ends.append(n)
    plan[channels] = ends[0]
    plan[channels + 1] = jnp.maximum(ends[0], ends[1] - ends[0])
    plan[channels + 2] = ends[1]
    plan[channels + 3] = dims[0]
    plan[channels + 4] = dims[1]
    for copy in copies:
        copy.wait()
    inverse[...] = 1.0 / inverse[...]


def bounds(plan):
    channels = plan.shape[0] - 5
    return plan[channels], plan[channels + 1], plan[channels + 2]


def mask_of(plan, rows, width, first=0):
    channels = plan.shape[0] - 5
    a = lax.broadcasted_iota(jnp.int32, (rows, width), 0) + first
    b = lax.broadcasted_iota(jnp.int32, (rows, width), 1)
    return (a < plan[channels + 3]) & (b < plan[channels + 4])


def fold(x):
    return jnp.sum(x.reshape(x.shape[0] // 8, 8, x.shape[1]), axis=0)


def lanes_of(values, lanes):
    lane = lax.broadcasted_iota(jnp.int32, (8, 128), 1)
    out = jnp.zeros((8, 128), F32)
    for value, at in zip(values, lanes):
        whole = jnp.sum(jnp.sum(value, axis=0, keepdims=True), axis=1, keepdims=True)
        out = jnp.where(lane == at, whole, out)
    return out


def first_kernel(
    plan, lb, nb, inv, l_hbm, r_hbm, x_ref, far_ref, head_sums, uu_ref,
    t_ref, l_buf, r_buf, sems,
):
    refs = (l_hbm, r_hbm, l_buf, r_buf, sems)
    head = bounds(plan)[1]

    def start(i, carry):
        for copy in env_copies(i, plan[i], refs):
            copy.start()
        return carry

    lax.fori_loop(0, head, start, 0)
    scaled = (lb[...].astype(F32) * inv[...].astype(F32)).astype(BF16)
    guess = jnp.dot(scaled, nb[...], preferred_element_type=F32)
    guess = jnp.where(mask_of(plan, *guess.shape), guess, 0.0)
    x_ref[...] = guess.astype(BF16)
    uu_ref[...] = lanes_of([fold(guess * guess)], [UU])

    def arrived(i):
        for copy in env_copies(i, plan[i], refs):
            copy.wait()
        return i

    apply_head(plan, x_ref, t_ref, head_sums, l_buf, r_buf, arrived)
    far_ref[...] = head_sums[0].astype(BF16)


def at(red, lane):
    return red[0:1, lane : lane + 1]


def scales_of(reds):
    return [lax.rsqrt(at(reds[0], UU) + EPS)] + [jnp.ones((1, 1), F32)] * (len(reds) - 1)


def solve_step(reds):
    k = len(reds) - 1
    s = scales_of(reds)
    red = reds[k]
    steps = range(k + 1)
    gram = {}
    for i in steps:
        for j in range(i + 1):
            gram[i, j] = gram[j, i] = s[i] * s[j] * at(reds[i], HX + j)
    column = [s[j] * s[k] * at(red, HV + j) for j in steps]
    theta = column[k]
    d = [s[j] * s[k] * (at(red, HA + j) - theta * at(red, HE + j)) for j in steps]
    cc = s[k] * s[k] * (at(red, AA) - 2.0 * theta * at(red, AE) + theta * theta * at(red, EE))
    pp = cc
    for i in steps:
        pp = pp - 2.0 * d[i] * d[i]
        for j in steps:
            pp = pp + d[i] * d[j] * gram[i, j]
    norm = lax.rsqrt(jnp.maximum(pp, 0.0) + EPS)
    return column, norm * s[k], norm * s[k] * theta, [norm * d[j] * s[j] for j in steps]


def following(reds, image, inverse, basis, out):
    _, w_v, w_x, w = solve_step(reds)
    k = len(reds) - 1

    def body(block, carry):
        rows = pl.ds(block * ROWS, ROWS)
        xs = [b[rows, :].astype(F32) for b in basis]
        p = (image[rows, :] * w_v - xs[k] * w_x) * inverse[rows, :]
        for j in range(k + 1):
            p = p - xs[j] * w[j]
        out[rows, :] = p.astype(BF16)
        return carry

    lax.fori_loop(0, out.shape[0] // ROWS, body, 0)


def next_kernel(k, scale, *refs):
    plan, got = refs[:2]
    older = refs[2 : 1 + k]
    basis = refs[1 + k : 1 + 2 * k]
    image, inverse, l_ref, r_ref, x_ref, far_ref, head_sums, red_ref, t_ref = refs[1 + 2 * k :]
    red_ref[...] = summed(got, scale)
    reds = [r[...] for r in older] + [red_ref[...]]
    following(reds, image, inverse, basis, x_ref)
    apply_head(plan, x_ref, t_ref, head_sums, l_ref, r_ref)
    far_ref[...] = head_sums[0].astype(BF16)


def summed(got, scale):
    return jnp.broadcast_to(jnp.sum(got[...], axis=0) * scale, (8, 128))


def last_kernel(scale, *refs):
    k = MATVECS
    got = refs[0]
    older = refs[1:k]
    basis = refs[k : 2 * k]
    image, inverse, x_hbm, image_hbm, projected, x_buf, sems = refs[2 * k :]
    out = pltpu.make_async_copy(image, image_hbm, sems.at[0])
    out.start()
    reds = [r[...] for r in older] + [summed(got, scale)]
    following(reds, image, inverse, basis, x_buf)
    new = pltpu.make_async_copy(x_buf, x_hbm, sems.at[1])
    new.start()
    row = lax.broadcasted_iota(jnp.int32, (MATVECS, MATVECS), 0)
    col = lax.broadcasted_iota(jnp.int32, (MATVECS, MATVECS), 1)
    table = jnp.zeros((MATVECS, MATVECS), F32)
    for step in range(MATVECS):
        column = solve_step(reds[: step + 1])[0]
        for j in range(step + 1):
            table = jnp.where((row == j) & (col == step), column[j], table)
    projected[...] = table
    new.wait()
    out.wait()


def near_kernel(plan, x, head_sums, l_ref, r_ref, near_ref, t_ref, acc):
    _, head, split = bounds(plan)
    acc[...] = head_sums[1]
    apply_channels(plan, head, split, x, t_ref, acc, l_ref, r_ref)
    near_ref[...] = acc[...].astype(BF16)


def stay_kernel(k, plan, *refs):
    basis = refs[: k + 1]
    inverse, l_ref, r_ref, stay_ref, dots_ref, t_ref = refs[k + 1 :]
    split = bounds(plan)[2]
    width = stay_ref.shape[1]
    stay_ref[...] = jnp.zeros_like(stay_ref)
    apply_channels(plan, split, l_ref.shape[0], basis[k], t_ref, stay_ref, l_ref, r_ref)

    def body(block, sums):
        rows = pl.ds(block * ROWS, ROWS)
        xs = [b[rows, :].astype(F32) for b in basis]
        e = xs[k] * inverse[rows, :]
        new = [x * e for x in xs] + [x * xs[k] for x in xs] + [e * e]
        return tuple(total + fold(x) for total, x in zip(sums, new))

    zero = tuple(jnp.zeros((8, width), F32) for _ in range(2 * k + 3))
    sums = lax.fori_loop(0, stay_ref.shape[0] // ROWS, body, zero)
    lanes = [HE + j for j in range(k + 1)] + [HX + j for j in range(k + 1)] + [EE]
    dots_ref[...] = lanes_of(sums, lanes)


def joined_kernel(stay, from_far, out):
    out[...] = stay[...] + from_far[...].astype(F32)


def image_kernel(k, plan, *refs):
    basis = refs[: k + 1]
    stay, from_near, inverse, dots = refs[k + 1 : k + 5]
    rest = refs[k + 5 :]
    if k == 0:
        guess_dots, image, out = rest
    else:
        image, out = rest
    width = stay.shape[1]

    def body(block, sums):
        rows = pl.ds(block * ROWS, ROWS)
        v = stay[rows, :] + from_near[rows, :].astype(F32)
        v = jnp.where(mask_of(plan, ROWS, width, block * ROWS), v, 0.0)
        image[rows, :] = v
        xs = [b[rows, :].astype(F32) for b in basis]
        d = inverse[rows, :]
        a = v * d
        e = xs[k] * d
        new = [x * v for x in xs] + [x * a for x in xs] + [a * a, a * e]
        return tuple(total + fold(x) for total, x in zip(sums, new))

    zero = tuple(jnp.zeros((8, width), F32) for _ in range(2 * k + 4))
    sums = lax.fori_loop(0, stay.shape[0] // ROWS, body, zero)
    lanes = [HV + j for j in range(k + 1)] + [HA + j for j in range(k + 1)] + [AA, AE]
    total = lanes_of(sums, lanes) + dots[...]
    if k == 0:
        total = total + guess_dots[...]
    out[...] = jnp.broadcast_to(total[None, : out.shape[1]], out.shape)


def call(kernel, args, specs, outs, out_specs, scratch, flops, limit):
    return pl.pallas_call(
        kernel,
        out_shape=[jax.ShapeDtypeStruct(*o) for o in outs],
        in_specs=specs,
        out_specs=out_specs,
        scratch_shapes=scratch,
        compiler_params=pltpu.CompilerParams(vmem_limit_bytes=limit * MIB),
        cost_estimate=pl.CostEstimate(
            flops=flops, bytes_accessed=4 * MIB + flops // 512, transcendentals=0
        ),
    )(*args)


def in_hbm(*arrays):
    return [pltpu.with_memory_space_constraint(x, pltpu.HBM) for x in arrays]


def swapped(block, pairs):
    return lax.ppermute(block, "sec", pairs)


def per_device(
    left_env, right_env, left_block, right_block, inv_sv, precond, sector_dims, channel_charge
):
    width = left_block.shape[-1]
    sectors = lax.axis_size("sec")
    segments = lax.axis_size("seg")
    channels = left_env.shape[2]
    scale = 1.0 / (sectors * width * width)
    lenv, renv = left_env[0, 0], right_env[0, 0]
    dims = sector_dims[0, 0]
    odd = lax.rem(lax.axis_index("sec"), 2)
    far = (2 * odd - 1).astype(jnp.int32).reshape(1)
    far_pairs = [(i, i + 1) for i in range(1, sectors - 1, 2)]
    far_pairs += [(j, i) for i, j in far_pairs]
    near_pairs = [(i, i + 1) for i in range(0, sectors, 2)]
    near_pairs += [(j, i) for i, j in near_pairs]
    route = [((i + 1) % segments, i) for i in range(segments)]
    nb, inv = lax.ppermute((right_block[0, 0], inv_sv[0]), "seg", route)

    square = (width, width)
    small = ((8, 128), F32)
    one = 4 * width**3 * channels // 3
    left, inverse, plan = call(
        prepare_kernel,
        (channel_charge, far, dims, *in_hbm(left_block[0, 0], precond[0, 0])),
        [SMEM] * 3 + [HBM] * 2,
        [(square, BF16), (square, F32), ((channels + 5,), jnp.int32)],
        [VMEM, VMEM, SMEM],
        [pltpu.SemaphoreType.DMA((2,))], MIB, 8,
    )
    scratch = [pltpu.VMEM((2, width, width), BF16), pltpu.VMEM(square, F32)]
    head_scratch = [pltpu.VMEM((GROUP, width, width), BF16)]
    buffers = [pltpu.VMEM(lenv.shape, BF16)] * 2 + [pltpu.SemaphoreType.DMA((channels, 2))]
    basis, reds = [], []
    for k in range(MATVECS):
        outs = [(square, BF16), (square, BF16), ((2, width, width), F32), small]
        if k == 0:
            x, to_far, head_sums, guess_dots = call(
                first_kernel,
                (plan, left, nb, inv, *in_hbm(lenv, renv)),
                [SMEM] + [VMEM] * 3 + [HBM] * 2,
                outs, [VMEM] * 4, head_scratch + buffers, 20 * one, 24,
            )
        else:
            x, to_far, head_sums, red = call(
                functools.partial(next_kernel, k, scale),
                (plan, got, *reds, *basis, image, inverse, lenv, renv),
                [SMEM] + [VMEM] * (2 * k + 4),
                outs, [VMEM] * 4, head_scratch, one, 16,
            )
            reds.append(red)
        basis.append(x)
        from_far = swapped(to_far, far_pairs)
        (to_near,) = call(
            near_kernel, (plan, x, head_sums, lenv, renv), [SMEM] + [VMEM] * 4,
            [(square, BF16)], [VMEM], scratch, one, 16,
        )
        from_near = swapped(to_near, near_pairs)
        stay, dots = call(
            functools.partial(stay_kernel, k),
            (plan, *basis, inverse, lenv, renv),
            [SMEM] + [VMEM] * (k + 4),
            [(square, F32), small], [VMEM] * 2,
            scratch[:1], one, 16,
        )
        (stay,) = call(
            joined_kernel, (stay, from_far), [VMEM] * 2, [(square, F32)], [VMEM], [], MIB, 16
        )
        extra = (guess_dots,) if k == 0 else ()
        image, spread = call(
            functools.partial(image_kernel, k),
            (plan, *basis, stay, from_near, inverse, dots, *extra),
            [SMEM] + [VMEM] * (k + 5 + len(extra)),
            [(square, F32), ((sectors, ROW, 128), F32)], [VMEM] * 2,
            [], MIB, 16,
        )
        got = lax.all_to_all(spread, "sec", 0, 0)
    x, image, projected = call(
        functools.partial(last_kernel, scale),
        (got, *reds, *basis, image, inverse),
        [VMEM] * (2 * MATVECS + 2),
        [(square, BF16), (square, F32), ((MATVECS, MATVECS), F32)], [HBM, HBM, VMEM],
        [pltpu.VMEM(square, BF16), pltpu.SemaphoreType.DMA((2,))], MIB, 16,
    )
    return (x[None, None], image[None, None], projected[None])


def solution(mesh):
    in_specs = (
        P("seg", "sec", None, None, None),
        P("seg", "sec", None, None, None),
        P("seg", "sec", None, None),
        P("seg", "sec", None, None),
        P("seg", "sec", None),
        P("seg", "sec", None, None),
        P("seg", "sec", None),
        P(),
    )
    out_specs = (P("seg", "sec", None, None), P("seg", "sec", None, None), P("seg", None, None))
    return jax.shard_map(
        per_device, mesh=mesh, in_specs=in_specs, out_specs=out_specs, check_vma=False
    )
```
